256 devices in a mesh: row: 16 (over x, y_hi, core), col: 16 (over z, y_lo).
Axes of the slice: x: 4, y: 4 (y_hi: 2, y_lo: 2; y = y_hi * 2 + y_lo), z: 8, core: 2. Of those that a mesh axis runs over, the one named last changes fastest.
Arguments:
- activations: bfloat16 [1024, 8192], P(None, 'row'), may hold values from -10 to 10
- cotangents: bfloat16 [1024, 8192], P(None, 'row'), may hold values from -10 to 10
- act_factor: bfloat16 [8192, 8192], P('row', 'col'), may hold values from -0.5 to 1.5
- grad_factor: bfloat16 [8192, 8192], P('row', 'col'), may hold values from -0.5 to 1.5
Outputs:
- act_updated: bfloat16 [8192, 8192], P('row', 'col')
- grad_updated: bfloat16 [8192, 8192], P('row', 'col')
The draws below stay inside these ranges and needn't reach their ends.
All inputs are finite; a program needn't handle non-finite values.
Results may differ from the reference program's by a relative error of at most 0.0057.
Values may be sent and summed in bfloat16 or wider, within the bound.
No kernel may reach another device: no remote copies, remote signals or barrier semaphores. Data moves between devices by JAX's collectives and lax.ppermute only.
A program may use at most 64 MiB of HBM per device.

```python
import jax
import jax.numpy as jnp
from jax import lax

D = 8192
TOKENS = 1024


def factor_draw(key):
    first, second = jax.random.split(key)
    spread = jnp.clip(jax.random.normal(first, (D, D), jnp.float32), -4.0, 4.0)
    diag = jax.random.uniform(second, (D,), jnp.float32, 0.9, 1.1)
    unit = jnp.eye(D, dtype=jnp.float32)
    return unit * diag[None, :] + (1.0 - unit) * spread * (0.5 / jnp.sqrt(jnp.float32(D)))


def rows_draw(key):
    first, second = jax.random.split(key, 2)
    place = jnp.arange(TOKENS, dtype=jnp.float32) / jnp.float32(max(TOKENS - 1, 1))
    jitter = jax.random.uniform(second, (TOKENS,), jnp.float32)
    scale = 0.2 * jnp.power(10.0, 0.5 * place + 0.5 * jitter)
    base = jnp.clip(jax.random.normal(first, (TOKENS, D), jnp.float32), -4.0, 4.0)
    return base * scale[:, None]


def draw_activations(key, part):
    return rows_draw(jax.random.fold_in(key, 101)).astype(jnp.bfloat16)


def draw_cotangents(key, part):
    return rows_draw(jax.random.fold_in(key, 202)).astype(jnp.bfloat16)


def draw_act_factor(key, part):
    return factor_draw(jax.random.fold_in(key, 303)).astype(jnp.bfloat16)


def draw_grad_factor(key, part):
    return factor_draw(jax.random.fold_in(key, 404)).astype(jnp.bfloat16)


def setup_inputs(seed: int = 0) -> dict:
    keys = jax.random.split(jax.random.key(seed), 5)
    activations = draw_activations(jax.random.fold_in(keys[4], 71), 0)
    cotangents = draw_cotangents(jax.random.fold_in(keys[4], 71), 0)
    act_factor = draw_act_factor(jax.random.fold_in(keys[4], 71), 0)
    grad_factor = draw_grad_factor(jax.random.fold_in(keys[4], 71), 0)
    return {"activations": activations, "cotangents": cotangents, "act_factor": act_factor, "grad_factor": grad_factor}


keep_scale = 1.45
gram_scale = 0.5


def project(rows, factor):
    return jnp.dot(rows.astype(jnp.float32), factor.astype(jnp.float32), precision=lax.Precision.HIGHEST).astype(jnp.bfloat16)


def update(factor, projected, scale):
    factor32 = factor.astype(jnp.float32)
    proj32 = projected.astype(jnp.float32)
    image = jnp.dot(factor32, proj32.T, precision=lax.Precision.HIGHEST).astype(jnp.bfloat16)
    image = lax.optimization_barrier(image).astype(jnp.float32)
    change = jnp.dot(image, proj32, precision=lax.Precision.HIGHEST)
    return (keep_scale * factor32 - (gram_scale * scale / TOKENS) * change).astype(jnp.bfloat16)


def reference(activations, cotangents, act_factor, grad_factor):
    act_proj = project(activations, act_factor)
    grad_proj = project(cotangents, grad_factor)
    act_mean = jnp.sum(jnp.square(act_proj.astype(jnp.float32))) / (TOKENS * D)
    grad_mean = jnp.sum(jnp.square(grad_proj.astype(jnp.float32))) / (TOKENS * D)
    return update(act_factor, act_proj, grad_mean), update(grad_factor, grad_proj, act_mean)
```

```python
import jax
import jax.numpy as jnp
from jax import lax
from jax.sharding import Mesh, PartitionSpec as P

D = 8192
TOKENS = 1024
X, YH, CORE, Z, YL = 4, 2, 2, 8, 2
ROW = ("x", "yh", "core")
COL = ("z", "yl")

keep_scale = 1.45
gram_scale = 0.5

f32 = jnp.float32
bf16 = jnp.bfloat16


def dot(a, b):
    return jnp.dot(a, b, preferred_element_type=f32)


def dot_t(a, b):
    return lax.dot_general(a, b, (((1,), (1,)), ((), ())), preferred_element_type=f32)


def shift(a, axis, size, by=1):
    return lax.ppermute(a, axis, [(i, (i + by) % size) for i in range(size)])


def half(a, which):
    rows = a.shape[0] // 2
    return lax.dynamic_slice_in_dim(a, which * rows, rows, 0)


def reduce_direct(a, axes, n):
    parts = lax.all_to_all(a.astype(bf16).reshape(n, -1, a.shape[1]), axes, 0, 0, tiled=True)
    return jnp.sum(parts.astype(f32), axis=0).astype(bf16)


def gather_direct(a, axes, n):
    copies = jnp.broadcast_to(a[None], (n,) + a.shape)
    return lax.all_to_all(copies, axes, 0, 0, tiled=True).reshape(-1, a.shape[1])


def project(rows, factor):
    core = lax.axis_index("core")
    away = shift(dot(half(rows, 1 - core), factor).astype(bf16), "core", CORE)
    total = dot(half(rows, core), factor) + away.astype(f32)
    own = reduce_direct(total, ("x", "yh"), X * YH)
    mine = gather_direct(own, ("x", "yh"), X * YH)
    other = shift(mine, "core", CORE)
    return jnp.concatenate([mine, other], axis=0)


def image_of(factor, proj):
    yl = lax.axis_index("yl")
    away = shift(dot_t(half(factor, 1 - yl), proj).astype(bf16), "yl", YL)
    total = dot_t(half(factor, yl), proj) + away.astype(f32)
    own = reduce_direct(total, "z", Z)
    mine = gather_direct(own, "z", Z)
    other = shift(mine, "yl", YL)
    first = jnp.where(yl == 0, mine, other)
    second = jnp.where(yl == 0, other, mine)
    return jnp.concatenate([first, second], axis=0)


def col_sum(a):
    a = a + shift(a, "yl", YL)
    for by in (1, 2, 4):
        a = a + shift(a, "z", Z, by)
    return a


def local(activations, cotangents, act_factor, grad_factor):
    act_proj = project(activations, act_factor)
    grad_proj = project(cotangents, grad_factor)
    squares = jnp.stack(
        [jnp.sum(jnp.square(p.astype(f32))) for p in (act_proj, grad_proj)]
    )
    means = col_sum(jnp.broadcast_to(squares[:, None], (2, 128))) / (TOKENS * D)
    outs = []
    for factor, proj, mean in (
        (act_factor, act_proj, means[1, 0]),
        (grad_factor, grad_proj, means[0, 0]),
    ):
        change = dot(image_of(factor, proj), proj)
        outs.append(
            (keep_scale * factor.astype(f32) - gram_scale * mean / TOKENS * change).astype(bf16)
        )
    return tuple(outs)


def solution(mesh):
    fine = Mesh(mesh.devices.reshape(X, YH, CORE, Z, YL), ROW + COL)
    return jax.shard_map(
        local,
        mesh=fine,
        in_specs=(P(None, ROW), P(None, ROW), P(ROW, COL), P(ROW, COL)),
        out_specs=(P(ROW, COL), P(ROW, COL)),
        check_vma=False,
    )
```

```python
import jax
import jax.numpy as jnp
from jax import lax
from jax.sharding import Mesh, PartitionSpec as P

D = 8192
TOKENS = 1024
X, YH, CORE, Z, YL = 4, 2, 2, 8, 2
ROW = ("x", "yh", "core")
COL = ("z", "yl")

keep_scale = 1.45
gram_scale = 0.5

f32 = jnp.float32
bf16 = jnp.bfloat16


def dot(a, b):
    return jnp.dot(a, b, preferred_element_type=f32)


def dot_t(a, b):
    return lax.dot_general(a, b, (((1,), (1,)), ((), ())), preferred_element_type=f32)


def shift(a, axis, size, by=1):
    return lax.ppermute(a, axis, [(i, (i + by) % size) for i in range(size)])


def piece(a, index, rows):
    return lax.dynamic_slice_in_dim(a, index * rows, rows, 0)


def half(a, which):
    return piece(a, which, a.shape[0] // 2)


def add_up(first, parts):
    for part in parts:
        first = first + part.astype(f32)
    return first


def after(*arrays):
    return sum(jnp.minimum(jnp.abs(a.reshape(-1)[0].astype(f32)), 0.0) for a in arrays)


def core_sum(rows, factor):
    core = lax.axis_index("core")
    away = shift(dot(half(rows, 1 - core), factor).astype(bf16), "core", CORE)
    return dot(half(rows, core), factor) + away.astype(f32)


def x_parts(total):
    x = lax.axis_index("x")
    size = total.shape[0] // X
    return [
        shift(piece(total, lax.rem(x + by, X), size).astype(bf16), "x", X, by)
        for by in range(1, X)
    ]


def gathered(total, parts):
    x, yh = lax.axis_index("x"), lax.axis_index("yh")
    total = add_up(piece(total, x, total.shape[0] // X), parts)
    away = shift(half(total, 1 - yh).astype(bf16), "yh", YH)
    own = (half(total, yh) + away.astype(f32)).astype(bf16)
    pair = jnp.concatenate([own, shift(own, "yh", YH)], axis=0)
    mine = jnp.concatenate([pair] + [shift(pair, "x", X, by) for by in range(1, X)], axis=0)
    return jnp.concatenate([mine, shift(mine, "core", CORE)], axis=0)


def image_sum(factor, proj):
    yl = lax.axis_index("yl")
    away = shift(dot_t(half(factor, 1 - yl), proj).astype(bf16), "yl", YL)
    return dot_t(half(factor, yl), proj) + away.astype(f32)


def reduce_z(a):
    parts = lax.all_to_all(a.astype(bf16).reshape(Z, -1, a.shape[1]), "z", 0, 0, tiled=True)
    return add_up(parts[0].astype(f32), [parts[k] for k in range(1, Z)]).astype(bf16)


def gather_z(a):
    copies = jnp.broadcast_to(a[None], (Z,) + a.shape)
    return lax.all_to_all(copies, "z", 0, 0, tiled=True).reshape(-1, a.shape[1])


def whole_image(mine):
    yl = lax.axis_index("yl")
    other = shift(mine, "yl", YL)
    first = jnp.where(yl == 0, mine, other)
    second = jnp.where(yl == 0, other, mine)
    return jnp.concatenate([first, second], axis=0)


def col_sum(a):
    a = a + shift(a, "yl", YL)
    for by in (1, 2, 4):
        a = a + shift(a, "z", Z, by)
    return a


def updated(factor, image, proj, mean):
    change = dot(image, proj)
    return (keep_scale * factor.astype(f32) - gram_scale * mean / TOKENS * change).astype(bf16)


def local(activations, cotangents, act_factor, grad_factor):
    act_total = core_sum(activations, act_factor)
    act_parts = x_parts(act_total)
    grad_total = core_sum(cotangents, grad_factor) + after(*act_parts)
    grad_parts = x_parts(grad_total)
    act_proj = gathered(act_total, act_parts)
    grad_proj = gathered(grad_total, grad_parts)
    squares = [jnp.sum(jnp.square(p.astype(f32))) for p in (act_proj, grad_proj)]
    row = lax.broadcasted_iota(jnp.int32, (8, 128), 0)
    means = col_sum(jnp.where(row == 0, squares[0], squares[1])) / (TOKENS * D)
    act_own = reduce_z(image_sum(act_factor, act_proj))
    grad_own = reduce_z(image_sum(grad_factor, grad_proj) + after(means))
    act_image = whole_image(gather_z(act_own))
    grad_image = whole_image(gather_z(grad_own))
    return (
        updated(act_factor, act_image, act_proj, means[1, 0]),
        updated(grad_factor, grad_image, grad_proj, means[0, 0]),
    )


def solution(mesh):
    fine = Mesh(mesh.devices.reshape(X, YH, CORE, Z, YL), ROW + COL)
    return jax.shard_map(
        local,
        mesh=fine,
        in_specs=(P(None, ROW), P(None, ROW), P(ROW, COL), P(ROW, COL)),
        out_specs=(P(ROW, COL), P(ROW, COL)),
        check_vma=False,
    )
```

```python
import jax
import jax.numpy as jnp
from jax import lax
from jax.experimental import pallas as pl
from jax.experimental.pallas import tpu as pltpu
from jax.sharding import Mesh, PartitionSpec as P

D = 8192
TOKENS = 1024
X, YH, CORE, Z, YL = 4, 2, 2, 8, 2
ROW = ("x", "yh", "core")
COL = ("z", "yl")
ROWS = D // (X * YH * CORE)
WIDTH = D // (Z * YL)
HALF = TOKENS // CORE
SMALL = 256
LARGE = TOKENS - SMALL
PART = ROWS // (Z * YL)

keep_scale = 1.45
gram_scale = 0.5

f32 = jnp.float32
bf16 = jnp.bfloat16


def dot(a, b):
    return jnp.dot(a, b, preferred_element_type=f32)


def dot_t(a, b):
    return lax.dot_general(a, b, (((1,), (1,)), ((), ())), preferred_element_type=f32)


def shift(a, axis, size, by=1):
    return lax.ppermute(a, axis, [(i, (i + by) % size) for i in range(size)])


def kernel_call(body, outs, *args, index=None, unread=(), flops=0):
    specs = [pl.BlockSpec(memory_space=pltpu.VMEM)] * len(args)
    specs += [pl.BlockSpec(memory_space=pl.ANY)] * len(unread)
    if index is not None:
        specs = [pl.BlockSpec(memory_space=pltpu.SMEM)] + specs
        args = (index.astype(jnp.int32).reshape(1),) + args
    size = sum(a.size * a.dtype.itemsize for a in args)
    return pl.pallas_call(
        body,
        out_shape=[jax.ShapeDtypeStruct(shape, dtype) for shape, dtype in outs],
        in_specs=specs,
        out_specs=[pl.BlockSpec(memory_space=pltpu.VMEM)] * len(outs),
        compiler_params=pltpu.CompilerParams(vmem_limit_bytes=48 * 2**20),
        cost_estimate=pl.CostEstimate(flops=flops, bytes_accessed=size, transcendentals=0),
    )(*args, *unread)


def project_away(which, acts, cots, act_factor, grad_factor, out):
    rows = pl.ds(pl.multiple_of(which[0] * HALF, HALF), HALF)
    out[:, :WIDTH] = dot(acts[rows, :], act_factor[...]).astype(bf16)
    out[:, WIDTH:] = dot(cots[rows, :], grad_factor[...]).astype(bf16)


def project_own(which, acts, cots, act_factor, grad_factor, came, out):
    rows = pl.ds(pl.multiple_of(which[0] * HALF, HALF), HALF)
    for rows_ref, factor, start in ((acts, act_factor, 0), (cots, grad_factor, WIDTH)):
        cols = slice(start, start + WIDTH)
        total = dot(rows_ref[rows, :], factor[...]) + came[:, cols].astype(f32)
        out[:, cols] = total.astype(bf16)


def project_sum(parts, copies, squares):
    total = parts[0].astype(f32)
    for k in range(1, X * YH):
        total = total + parts[k].astype(f32)
    own = total.astype(bf16)
    for k in range(X * YH):
        copies[k] = own
    own = jnp.square(own.astype(f32))
    row = lax.broadcasted_iota(jnp.int32, (8, 128), 0)
    squares[...] = jnp.where(row == 0, jnp.sum(own[:, :WIDTH]), jnp.sum(own[:, WIDTH:]))


def factor_columns(f):
    return slice(f * WIDTH, (f + 1) * WIDTH)


def image_small(act_factor, grad_factor, mine, _, out):
    for f, factor in enumerate((act_factor, grad_factor)):
        image = dot_t(factor[...].reshape(ROWS, WIDTH), mine[:SMALL, factor_columns(f)])
        out[:, f] = image.astype(bf16).reshape(Z, YL * PART, SMALL)


def half_image(factor, which, mine, other, f):
    rows = factor[:, pl.ds(which, 1)].reshape(ROWS // YL, WIDTH)
    return (
        dot_t(rows, mine[SMALL:, factor_columns(f)]),
        dot_t(rows, other[:, factor_columns(f)]),
    )


def image_away(which, act_factor, grad_factor, mine, other, out):
    for f, factor in enumerate((act_factor, grad_factor)):
        first, second = half_image(factor, which[0], mine, other, f)
        out[f, :, : HALF - SMALL] = first.astype(bf16)
        out[f, :, HALF - SMALL :] = second.astype(bf16)


def image_own(which, act_factor, grad_factor, mine, other, came, _, out):
    cut = HALF - SMALL
    for f, factor in enumerate((act_factor, grad_factor)):
        first, second = half_image(factor, which[0], mine, other, f)
        first = (first + came[f, :, :cut].astype(f32)).astype(bf16)
        second = (second + came[f, :, cut:].astype(f32)).astype(bf16)
        out[:, f, :, :cut] = first.reshape(Z, PART, cut)
        out[:, f, :, cut:] = second.reshape(Z, PART, LARGE - cut)


def small_sum(which, parts, away, own):
    def total(side):
        out = parts[0, :, pl.ds(side, 1)].astype(f32)
        for k in range(1, Z):
            out = out + parts[k, :, pl.ds(side, 1)].astype(f32)
        return out.reshape(2, PART, SMALL)

    own[...] = total(which[0])
    away[...] = total(1 - which[0]).astype(bf16)


def small_copies(own, other, _, copies):
    for k in range(Z):
        copies[k, 0] = own[...]
        copies[k, 1] = other[...]


def large_sum(parts, _, copies):
    total = parts[0].astype(f32)
    for k in range(1, Z):
        total = total + parts[k].astype(f32)
    own = total.astype(bf16)
    for k in range(Z):
        copies[k] = own


def update(which, squares, act_factor, grad_factor, mine, other, own_large, other_large, small, act_out, grad_out):
    cut = HALF - SMALL
    for f, (factor, out) in enumerate(((act_factor, act_out), (grad_factor, grad_out))):
        scale = squares[1 - f : 2 - f, :1] / (TOKENS * D) * (gram_scale / TOKENS)
        for side, large in enumerate((own_large, other_large)):
            where = pl.ds(which[0] if side == 0 else 1 - which[0], 1)
            image = large[:, f].reshape(ROWS // YL, LARGE)
            change = dot(image[:, :cut], mine[SMALL:, factor_columns(f)])
            change += dot(image[:, cut:], other[:, factor_columns(f)])
            image = small[:, side, f].reshape(ROWS // YL, SMALL)
            change += dot(image, mine[:SMALL, factor_columns(f)])
            kept = factor[:, where].reshape(ROWS // YL, WIDTH).astype(f32)
            new = (keep_scale * kept - scale * change).astype(bf16)
            out[:, where] = new.reshape(Z, 1, PART, WIDTH)


def local(activations, cotangents, act_factor, grad_factor):
    core, yl = lax.axis_index("core"), lax.axis_index("yl")
    product = 4 * HALF * ROWS * WIDTH
    given = (activations, cotangents, act_factor, grad_factor)
    (away,) = kernel_call(project_away, [((HALF, 2 * WIDTH), bf16)], *given, index=1 - core, flops=product)
    came = shift(away, "core", CORE)
    (total,) = kernel_call(project_own, [((HALF, 2 * WIDTH), bf16)], *given, came, index=core, flops=product)
    group = X * YH
    chunks = (group, HALF // group, 2 * WIDTH)
    parts = lax.all_to_all(total.reshape(chunks), ("x", "yh"), 0, 0, tiled=True)
    copies, squares = kernel_call(project_sum, [(chunks, bf16), ((8, 128), f32)], parts)
    mine = lax.all_to_all(copies, ("x", "yh"), 0, 0, tiled=True).reshape(HALF, 2 * WIDTH)
    for by in (1, 2, 4):
        squares = squares + shift(squares, "z", Z, by)
    other = shift(mine, "core", CORE)

    factors = [f.reshape(Z, YL, PART, WIDTH) for f in (act_factor, grad_factor)]
    (part,) = kernel_call(image_small, [((Z, 2, YL * PART, SMALL), bf16)], *factors, mine, unread=(squares,), flops=product // 2)
    small_parts = lax.all_to_all(part, "z", 0, 0, tiled=True)
    for axis, size, by in (("x", X, 1), ("x", X, 2), ("core", CORE, 1), ("yh", YH, 1), ("yl", YL, 1)):
        squares = squares + shift(squares, axis, size, by)
    (away,) = kernel_call(image_away, [((2, ROWS // YL, LARGE), bf16)], *factors, mine, other, index=1 - yl, flops=product // 2)
    came = shift(away, "yl", YL)
    (part,) = kernel_call(image_own, [((Z, 2, PART, LARGE), bf16)], *factors, mine, other, came, index=yl, unread=(small_parts,), flops=product // 2)
    shape = (2, PART, SMALL)
    away, own = kernel_call(small_sum, [(shape, bf16), (shape, f32)], small_parts.reshape(Z, 2, YL, PART, SMALL), index=yl)
    large_parts = lax.all_to_all(part, "z", 0, 0, tiled=True)
    own = (own + shift(away, "yl", YL).astype(f32)).astype(bf16)
    from_other = shift(own, "yl", YL)
    (copies,) = kernel_call(large_sum, [((Z, 2, PART, LARGE), bf16)], large_parts, unread=(squares,))
    own_large = lax.all_to_all(copies, "z", 0, 0, tiled=True)
    (copies,) = kernel_call(small_copies, [((Z, YL) + shape, bf16)], own, from_other, unread=(own_large,))
    small = lax.all_to_all(copies, "z", 0, 0, tiled=True)
    other_large = shift(own_large, "yl", YL)
    outs = kernel_call(
        update, [((Z, YL, PART, WIDTH), bf16)] * 2, squares, *factors, mine, other, own_large, other_large, small, index=yl, flops=2 * product
    )
    return tuple(out.reshape(ROWS, WIDTH) for out in outs)


def solution(mesh):
    fine = Mesh(mesh.devices.reshape(X, YH, CORE, Z, YL), ROW + COL)
    return jax.shard_map(
        local,
        mesh=fine,
        in_specs=(P(None, ROW), P(None, ROW), P(ROW, COL), P(ROW, COL)),
        out_specs=(P(ROW, COL), P(ROW, COL)),
        check_vma=False,
    )
```

```python
import jax
import jax.numpy as jnp
from jax import lax
from jax.experimental import pallas as pl
from jax.experimental.pallas import tpu as pltpu
from jax.sharding import Mesh, PartitionSpec as P

D = 8192
TOKENS = 1024
X, YH, CORE, Z, YL = 4, 2, 2, 8, 2
ROW = ("x", "yh", "core")
COL = ("z", "yl")
ROWS = D // (X * YH * CORE)
WIDTH = D // (Z * YL)
HALF = TOKENS // CORE
PART = ROWS // (Z * YL)

REDUCE = (4, -3, 3, -2, 2, -1, 1, 0)
GATHER = (0, -1, 1, -2, 2, -3, 3, -4)

keep_scale = 1.45
gram_scale = 0.5

f32 = jnp.float32
bf16 = jnp.bfloat16


def dot(a, b):
    return jnp.dot(a, b, preferred_element_type=f32)


def dot_t(a, b):
    return lax.dot_general(a, b, (((1,), (1,)), ((), ())), preferred_element_type=f32)


def shift(a, axis, size, by=1):
    return lax.ppermute(a, axis, [(i, (i + by) % size) for i in range(size)])


def kernel_call(body, outs, *args, index=None, unread=(), flops=0, spec=pl.BlockSpec(memory_space=pltpu.VMEM)):
    specs = [spec] * len(args)
    specs += [pl.BlockSpec(memory_space=pl.ANY)] * len(unread)
    if index is not None:
        specs = [pl.BlockSpec(memory_space=pltpu.SMEM)] + specs
        args = (jnp.stack([i.astype(jnp.int32) for i in index]),) + args
    size = sum(a.size * a.dtype.itemsize for a in args)
    return pl.pallas_call(
        body,
        out_shape=[jax.ShapeDtypeStruct(shape, dtype) for shape, dtype in outs],
        in_specs=specs,
        out_specs=[pl.BlockSpec(memory_space=pltpu.VMEM)] * len(outs),
        compiler_params=pltpu.CompilerParams(vmem_limit_bytes=48 * 2**20),
        cost_estimate=pl.CostEstimate(flops=flops, bytes_accessed=size, transcendentals=0),
    )(*args, *unread)


def tied(a, other):
    anywhere = pl.BlockSpec(memory_space=pl.ANY)
    return pl.pallas_call(
        lambda *refs: None,
        out_shape=jax.ShapeDtypeStruct(a.shape, a.dtype),
        in_specs=[anywhere, anywhere],
        out_specs=anywhere,
        input_output_aliases={0: 0},
    )(a, other)


def project_away(which, acts, cots, act_factor, grad_factor, out):
    rows = pl.ds(pl.multiple_of(which[0] * HALF, HALF), HALF)
    out[:, :WIDTH] = dot(acts[rows, :], act_factor[...]).astype(bf16)
    out[:, WIDTH:] = dot(cots[rows, :], grad_factor[...]).astype(bf16)


def project_own(which, acts, cots, act_factor, grad_factor, came, out):
    rows = pl.ds(pl.multiple_of(which[0] * HALF, HALF), HALF)
    for rows_ref, factor, start in ((acts, act_factor, 0), (cots, grad_factor, WIDTH)):
        cols = slice(start, start + WIDTH)
        total = dot(rows_ref[rows, :], factor[...]) + came[:, cols].astype(f32)
        out[:, cols] = total.astype(bf16)


def project_sum(parts, copies, squares):
    total = parts[0].astype(f32)
    for k in range(1, X * YH):
        total = total + parts[k].astype(f32)
    own = total.astype(bf16)
    for k in range(X * YH):
        copies[k] = own
    own = jnp.square(own.astype(f32))
    row = lax.broadcasted_iota(jnp.int32, (8, 128), 0)
    squares[...] = jnp.where(row == 0, jnp.sum(own[:, :WIDTH]), jnp.sum(own[:, WIDTH:]))


def factor_columns(f):
    return slice(f * WIDTH, (f + 1) * WIDTH)


def image_rows(factor, z, side, mine, other, f):
    rows = [factor[pl.ds(lax.rem(z + (e + Z), Z), 1), pl.ds(side, 1)].reshape(PART, WIDTH) for e in REDUCE]
    rows = jnp.concatenate(rows, axis=0)
    return (
        dot_t(rows, mine[:, factor_columns(f)]),
        dot_t(rows, other[:, factor_columns(f)]),
    )


def image_away(at, act_factor, grad_factor, mine, other, *outs):
    for f, factor in enumerate((act_factor, grad_factor)):
        first, second = image_rows(factor, at[0], 1 - at[1], mine, other, f)
        for k in range(Z):
            rows = slice(k * PART, (k + 1) * PART)
            outs[k // 2][k % 2, f, :, :HALF] = first[rows].astype(bf16)
            outs[k // 2][k % 2, f, :, HALF:] = second[rows].astype(bf16)


def image_own(at, act_factor, grad_factor, mine, other, *outs):
    for f, factor in enumerate((act_factor, grad_factor)):
        first, second = image_rows(factor, at[0], at[1], mine, other, f)
        for k in range(Z):
            rows = slice(k * PART, (k + 1) * PART)
            outs[k][f, :, :HALF] = first[rows]
            outs[k][f, :, HALF:] = second[rows]


def last_sum(own, away, up, down, _, out):
    total = own[...] + away[1].astype(f32) + up[...].astype(f32) + down[...].astype(f32)
    out[...] = total.astype(bf16)


def update(at, squares, act_factor, grad_factor, mine, other, *refs):
    chunks, outs = refs[: 2 * Z], refs[2 * Z :]
    for f, (factor, out) in enumerate(((act_factor, outs[0]), (grad_factor, outs[1]))):
        scale = squares[1 - f : 2 - f, :1] / (TOKENS * D) * (gram_scale / TOKENS)
        for side in range(YL):
            image = jnp.concatenate([c[f] for c in chunks[side * Z : (side + 1) * Z]], axis=0)
            change = dot(image[:, :HALF], mine[:, factor_columns(f)])
            change += dot(image[:, HALF:], other[:, factor_columns(f)])
            half = pl.ds(at[1] if side == 0 else 1 - at[1], 1)
            for k, e in enumerate(GATHER):
                place = (pl.ds(lax.rem(at[0] + (e + Z), Z), 1), half)
                kept = factor[place].reshape(PART, WIDTH).astype(f32)
                new = keep_scale * kept - scale * change[k * PART : (k + 1) * PART]
                out[place] = new.astype(bf16).reshape(1, 1, PART, WIDTH)


def local(activations, cotangents, act_factor, grad_factor):
    core, z, yl = (lax.axis_index(name) for name in ("core", "z", "yl"))
    product = 4 * HALF * ROWS * WIDTH
    given = (activations, cotangents, act_factor, grad_factor)
    sent = [((HALF, 2 * WIDTH), bf16)]
    (away,) = kernel_call(project_away, sent, *given, index=[1 - core], flops=product, spec=pl.BlockSpec())
    came = shift(away, "core", CORE)
    (total,) = kernel_call(project_own, sent, *given, came, index=[core], flops=product, spec=pl.BlockSpec())
    group = X * YH
    chunks = (group, HALF // group, 2 * WIDTH)
    parts = lax.all_to_all(total.reshape(chunks), ("x", "yh"), 0, 0, tiled=True)
    copies, squares = kernel_call(project_sum, [(chunks, bf16), ((8, 128), f32)], parts)
    mine = lax.all_to_all(copies, ("x", "yh"), 0, 0, tiled=True).reshape(HALF, 2 * WIDTH)
    for by in (1, 2, 4):
        squares = squares + shift(squares, "z", Z, by)
    mine = tied(mine, squares)
    other = shift(mine, "core", CORE)
    for axis, size, by in (("x", X, 1), ("x", X, 2), ("core", CORE, 1), ("yh", YH, 1), ("yl", YL, 1)):
        squares = squares + shift(squares, axis, size, by)

    factors = [f.reshape(Z, YL, PART, WIDTH) for f in (act_factor, grad_factor)]
    shape = (2, PART, TOKENS)
    sent = [((2,) + shape, bf16)] * (Z // 2)
    away = kernel_call(image_away, sent, *factors, mine, other, index=[z, yl], flops=product)
    away = [shift(a, "yl", YL) for a in away]
    own = kernel_call(image_own, [(shape, f32)] * Z, *factors, mine, other, index=[z, yl], flops=product)
    up, down = (own[k] + away[0][k].astype(f32) for k in (0, 1))
    for step in (1, 2, 3):
        up = shift(up.astype(bf16), "z", Z, 1)
        down = shift(down.astype(bf16), "z", Z, -1)
        up = own[2 * step] + away[step][0].astype(f32) + up.astype(f32)
        if step < 3:
            down = own[2 * step + 1] + away[step][1].astype(f32) + down.astype(f32)
    up = shift(up.astype(bf16), "z", Z, 1)
    (up,) = kernel_call(last_sum, [(shape, bf16)], own[7], away[3], up, down, unread=(squares,))
    down = up
    gathered = [up]
    for step in (1, 2, 3):
        up, down = shift(up, "z", Z, 1), shift(down, "z", Z, -1)
        gathered += [up, down]
    gathered.append(shift(up, "z", Z, 1))
    gathered += [shift(a, "yl", YL) for a in gathered]
    outs = kernel_call(
        update, [((Z, YL, PART, WIDTH), bf16)] * 2, squares, *factors, mine, other, *gathered, index=[z, yl], flops=2 * product
    )
    return tuple(out.reshape(ROWS, WIDTH) for out in outs)


def solution(mesh):
    fine = Mesh(mesh.devices.reshape(X, YH, CORE, Z, YL), ROW + COL)
    return jax.shard_map(
        local,
        mesh=fine,
        in_specs=(P(None, ROW), P(None, ROW), P(ROW, COL), P(ROW, COL)),
        out_specs=(P(ROW, COL), P(ROW, COL)),
        check_vma=False,
    )
```

```python
import jax
import jax.numpy as jnp
from jax import lax
from jax.experimental import pallas as pl
from jax.experimental.pallas import tpu as pltpu
from jax.sharding import Mesh, PartitionSpec as P

D = 8192
TOKENS = 1024
X, YH, CORE, Z, YL = 4, 2, 2, 8, 2
ROW = ("x", "yh", "core")
COL = ("z", "yl")
ROWS = D // (X * YH * CORE)
WIDTH = D // (Z * YL)
HALF = TOKENS // CORE
EXTRA = 128
PART = ROWS // (Z * YL)

REDUCE = (4, -3, 3, -2, 2, -1, 1, 0)
PLACES = ((0, 0), (1, 0), (1, 1), (2, 0), (2, 1), (3, 0), (3, 1), (4, 0))
GATHER = (0, -1, 1, -2, 2, -3, 3, -4)

keep_scale = 1.45
gram_scale = 0.5

f32 = jnp.float32
bf16 = jnp.bfloat16


def dot(a, b):
    return jnp.dot(a, b, preferred_element_type=f32)


def dot_t(a, b):
    return lax.dot_general(a, b, (((1,), (1,)), ((), ())), preferred_element_type=f32)


def shift(a, axis, size, by=1):
    return lax.ppermute(a, axis, [(i, (i + by) % size) for i in range(size)])


def kernel_call(body, outs, *args, index=None, flops=0, memory=pltpu.VMEM, scratch=(), room=48):
    specs = [pl.BlockSpec(memory_space=memory)] * len(args)
    if index is not None:
        specs = [pl.BlockSpec(memory_space=pltpu.SMEM)] + specs
        args = (jnp.stack([i.astype(jnp.int32) for i in index]),) + args
    size = sum(a.size * a.dtype.itemsize for a in args)
    return pl.pallas_call(
        body,
        out_shape=[jax.ShapeDtypeStruct(shape, dtype) for shape, dtype in outs],
        in_specs=specs,
        out_specs=[pl.BlockSpec(memory_space=pltpu.VMEM)] * len(outs),
        scratch_shapes=scratch,
        compiler_params=pltpu.CompilerParams(vmem_limit_bytes=room * 2**20),
        cost_estimate=pl.CostEstimate(flops=flops, bytes_accessed=size, transcendentals=0),
    )(*args)


def projected(which, given, bufs, sems):
    rows = pl.ds(pl.multiple_of(which[0] * HALF, HALF), HALF)
    refs = (given[0].at[rows], given[2], given[1].at[rows], given[3])
    copies = [pltpu.make_async_copy(r, buf, sems.at[i]) for i, (r, buf) in enumerate(zip(refs, bufs))]
    for copy in copies:
        copy.start()
    for f in range(2):
        copies[2 * f].wait()
        copies[2 * f + 1].wait()
        yield f, dot(bufs[2 * f][...], bufs[2 * f + 1][...])


def project(which, acts, cots, act_factor, grad_factor, out, *scratch):
    for f, total in projected(which, (acts, cots, act_factor, grad_factor), scratch[:4], scratch[4]):
        out[:, factor_columns(f)] = total.astype(out.dtype)


def project_sum(parts, copies):
    total = parts[0].astype(f32)
    for k in range(1, X * YH):
        total = total + parts[k].astype(f32)
    own = total.astype(bf16)
    for k in range(X * YH):
        copies[k] = own


def factor_columns(f):
    return slice(f * WIDTH, (f + 1) * WIDTH)


def image_rows(factor, z, side, mine, other, f):
    rows = [factor[pl.ds(lax.rem(z + (e + Z), Z), 1), pl.ds(side, 1)].reshape(PART, WIDTH) for e in REDUCE]
    rows = jnp.concatenate(rows, axis=0)
    return (
        dot_t(rows, mine[:, factor_columns(f)]),
        dot_t(rows, other[:, factor_columns(f)]),
    )


def image_away(at, act_factor, grad_factor, mine, other, *outs):
    for f, factor in enumerate((act_factor, grad_factor)):
        first, second = image_rows(factor, at[0], 1 - at[1], mine, other, f)
        for n, (group, k) in enumerate(PLACES):
            rows = slice(n * PART, (n + 1) * PART)
            outs[group][k, f, :, :HALF] = first[rows].astype(bf16)
            outs[group][k, f, :, HALF:] = second[rows].astype(bf16)


def image_own(at, act_factor, grad_factor, mine, other, *outs):
    for f, factor in enumerate((act_factor, grad_factor)):
        first, second = image_rows(factor, at[0], at[1], mine, other, f)
        for k in range(Z):
            rows = slice(k * PART, (k + 1) * PART)
            outs[k][f, :, :HALF] = first[rows]
            outs[k][f, :, HALF:] = second[rows]
        square = sum(jnp.square(part[:, factor_columns(f)].astype(f32)) for part in (mine, other))
        outs[Z][f : f + 1] = jnp.sum(square, axis=0, keepdims=True)


def last_sum(own, away, up, down, squares, out):
    total = own[...] + away[0].astype(f32) + up[...].astype(f32) + down[...].astype(f32)
    out[:, :, :TOKENS] = total.astype(bf16)
    row = lax.broadcasted_iota(jnp.int32, (PART, EXTRA), 0)
    for f in range(2):
        rest = jnp.full((PART, EXTRA), jnp.sum(squares[f : f + 1]))
        parts = jnp.zeros((PART, EXTRA), f32)
        for k in range(3):
            part = rest.astype(bf16).astype(f32)
            parts = jnp.where(row == k, part, parts)
            rest = rest - part
        out[f, :, TOKENS:] = parts.astype(bf16)


def changes(chunks, mine, other, f):
    image = jnp.concatenate([c[f, :, :TOKENS] for c in chunks], axis=0)
    change = dot(image[:, :HALF], mine[:, factor_columns(f)])
    return change + dot(image[:, HALF:], other[:, factor_columns(f)])


def own_changes(mine, other, *refs):
    chunks, (out, squares) = refs[:Z], refs[Z:]
    for f in range(2):
        out[f] = changes(chunks, mine, other, f)
        squares[f : f + 1] = share_sum(chunks, f)


def share_sum(chunks, f):
    return sum(jnp.sum(c[f, :, TOKENS:].astype(f32), axis=0, keepdims=True) for c in chunks)


def update(at, act_factor, grad_factor, mine, other, own_change, squares, *refs):
    chunks, outs = refs[:Z], refs[Z:]
    for f, (factor, out) in enumerate(((act_factor, outs[0]), (grad_factor, outs[1]))):
        total = squares[1 - f : 2 - f] + share_sum(chunks, 1 - f)
        scale = total[:, :1] / (TOKENS * D) * (gram_scale / TOKENS)
        for side in range(YL):
            change = own_change[f] if side == 0 else changes(chunks, mine, other, f)
            half = pl.ds(at[1] if side == 0 else 1 - at[1], 1)
            for k, e in enumerate(GATHER):
                place = (pl.ds(lax.rem(at[0] + (e + Z), Z), 1), half)
                kept = factor[place].reshape(PART, WIDTH).astype(f32)
                new = keep_scale * kept - scale * change[k * PART : (k + 1) * PART]
                out[place] = new.astype(bf16).reshape(1, 1, PART, WIDTH)


def after(a, *others):
    for other in others:
        a = a + jnp.minimum(jnp.abs(other), 0)
    return a


def local(activations, cotangents, act_factor, grad_factor):
    core, z, yl = (lax.axis_index(name) for name in ("core", "z", "yl"))
    product = 4 * HALF * ROWS * WIDTH
    given = (activations, cotangents, act_factor, grad_factor)
    scratch = [pltpu.VMEM((HALF, ROWS), bf16), pltpu.VMEM((ROWS, WIDTH), bf16)] * 2
    scratch.append(pltpu.SemaphoreType.DMA((4,)))
    setup = dict(flops=product, memory=pltpu.HBM, scratch=scratch, room=58)
    (away,) = kernel_call(project, [((HALF, 2 * WIDTH), bf16)], *given, index=[1 - core], **setup)
    came = shift(away, "core", CORE)
    (total,) = kernel_call(project, [((HALF, 2 * WIDTH), f32)], *given, index=[core], **setup)
    total = (total + came.astype(f32)).astype(bf16)
    group = X * YH
    chunks = (group, HALF // group, 2 * WIDTH)
    parts = lax.all_to_all(total.reshape(chunks), ("x", "yh"), 0, 0, tiled=True)
    (copies,) = kernel_call(project_sum, [(chunks, bf16)], parts)
    mine = lax.all_to_all(copies, ("x", "yh"), 0, 0, tiled=True).reshape(HALF, 2 * WIDTH)
    other = shift(mine, "core", CORE)

    factors = [f.reshape(Z, YL, PART, WIDTH) for f in (act_factor, grad_factor)]
    shape = (2, PART, TOKENS)
    sent = [((sum(g == group for g, _ in PLACES),) + shape, bf16) for group in range(5)]
    away = kernel_call(image_away, sent, *factors, mine, other, index=[z, yl], flops=product)
    away = [shift(a, "yl", YL) for a in away]
    *own, squares = kernel_call(
        image_own, [(shape, f32)] * Z + [((2, WIDTH), f32)], *factors, mine, other, index=[z, yl], flops=product
    )
    up = own[0] + away[0][0].astype(f32)
    down = own[1] + away[1][0].astype(f32)
    for step in (1, 2, 3):
        up = shift(up.astype(bf16), "z", Z, 1)
        up = own[2 * step] + away[step][1].astype(f32) + up.astype(f32)
        down = shift(down.astype(bf16), "z", Z, -1)
        if step < 3:
            down = own[2 * step + 1] + away[step + 1][0].astype(f32) + down.astype(f32)
    up = shift(up.astype(bf16), "z", Z, 1)
    shape = (2, PART, TOKENS + EXTRA)
    (up,) = kernel_call(last_sum, [(shape, bf16)], own[7], away[4], up, down, squares)

    down = up
    held, crossed = [up], [shift(up, "yl", YL)]
    for step in (1, 2, 3):
        if step == 3:
            up, down = after(up, crossed[0]), after(down, crossed[0])
        up, down = shift(up, "z", Z, 1), shift(down, "z", Z, -1)
        held += [up, down]
        crossed += [shift(up, "yl", YL), shift(down, "yl", YL)]
    up = shift(after(up, crossed[1], crossed[2]), "z", Z, 1)
    held.append(up)
    crossed.append(shift(up, "yl", YL))
    changed, squares = kernel_call(
        own_changes, [((2, ROWS // YL, WIDTH), f32), ((2, EXTRA), f32)], mine, other, *held, flops=product
    )
    outs = kernel_call(
        update, [((Z, YL, PART, WIDTH), bf16)] * 2, *factors, mine, other, changed, squares, *crossed, index=[z, yl], flops=product
    )
    return tuple(out.reshape(ROWS, WIDTH) for out in outs)


def solution(mesh):
    fine = Mesh(mesh.devices.reshape(X, YH, CORE, Z, YL), ROW + COL)
    return jax.shard_map(
        local,
        mesh=fine,
        in_specs=(P(None, ROW), P(None, ROW), P(ROW, COL), P(ROW, COL)),
        out_specs=(P(ROW, COL), P(ROW, COL)),
        check_vma=False,
    )
```

```python
import jax
import jax.numpy as jnp
from jax import lax
from jax.experimental import pallas as pl
from jax.experimental.pallas import tpu as pltpu
from jax.sharding import Mesh, PartitionSpec as P

D = 8192
TOKENS = 1024
X, YH, CORE, Z, YL = 4, 2, 2, 8, 2
ROW = ("x", "yh", "core")
COL = ("z", "yl")
ROWS = D // (X * YH * CORE)
WIDTH = D // (Z * YL)
HALF = TOKENS // CORE
EXTRA = 128
PART = ROWS // (Z * YL)

REDUCE = (-3, 3, 4, 2, -2, 1, -1, 0)
PLACES = ((0, 0), (0, 1), (1, 0), (1, 1), (1, 2), (2, 0), (2, 1), (2, 2))
GATHER = (0, -1, 1, -4, -2, 2, 3, -3)

keep_scale = 1.45
gram_scale = 0.5

f32 = jnp.float32
bf16 = jnp.bfloat16


def dot(a, b):
    return jnp.dot(a, b, preferred_element_type=f32)


def dot_t(a, b):
    return lax.dot_general(a, b, (((1,), (1,)), ((), ())), preferred_element_type=f32)


def shift(a, axis, size, by=1):
    return lax.ppermute(a, axis, [(i, (i + by) % size) for i in range(size)])


def add_up(first, parts):
    for part in parts:
        first = first + part.astype(f32)
    return first


def kernel_call(body, outs, *args, index=None, flops=0, memory=pltpu.VMEM, scratch=(), room=48):
    specs = [pl.BlockSpec(memory_space=memory)] * len(args)
    if index is not None:
        specs = [pl.BlockSpec(memory_space=pltpu.SMEM)] + specs
        args = (jnp.stack([i.astype(jnp.int32) for i in index]),) + args
    size = sum(a.size * a.dtype.itemsize for a in args)
    return pl.pallas_call(
        body,
        out_shape=[jax.ShapeDtypeStruct(shape, dtype) for shape, dtype in outs],
        in_specs=specs,
        out_specs=[pl.BlockSpec(memory_space=pltpu.VMEM)] * len(outs),
        scratch_shapes=scratch,
        compiler_params=pltpu.CompilerParams(vmem_limit_bytes=room * 2**20),
        cost_estimate=pl.CostEstimate(flops=flops, bytes_accessed=size, transcendentals=0),
    )(*args)


def projected(which, given, bufs, sems):
    rows = pl.ds(pl.multiple_of(which[0] * HALF, HALF), HALF)
    refs = (given[0].at[rows], given[2], given[1].at[rows], given[3])
    copies = [pltpu.make_async_copy(r, buf, sems.at[i]) for i, (r, buf) in enumerate(zip(refs, bufs))]
    for copy in copies:
        copy.start()
    for f in range(2):
        copies[2 * f].wait()
        copies[2 * f + 1].wait()
        yield f, dot(bufs[2 * f][...], bufs[2 * f + 1][...])


def project(which, acts, cots, act_factor, grad_factor, out, *scratch):
    for f, total in projected(which, (acts, cots, act_factor, grad_factor), scratch[:4], scratch[4]):
        out[:, factor_columns(f)] = total.astype(out.dtype)


def project_sum(parts, copies):
    total = parts[0].astype(f32)
    for k in range(1, X * YH):
        total = total + parts[k].astype(f32)
    own = total.astype(bf16)
    for k in range(X * YH):
        copies[k] = own


def factor_columns(f):
    return slice(f * WIDTH, (f + 1) * WIDTH)


def image_rows(factor, z, side, mine, other, f):
    rows = [factor[pl.ds(lax.rem(z + (e + Z), Z), 1), pl.ds(side, 1)].reshape(PART, WIDTH) for e in REDUCE]
    rows = jnp.concatenate(rows, axis=0)
    return (
        dot_t(rows, mine[:, factor_columns(f)]),
        dot_t(rows, other[:, factor_columns(f)]),
    )


def image_away(at, act_factor, grad_factor, mine, other, *outs):
    for f, factor in enumerate((act_factor, grad_factor)):
        first, second = image_rows(factor, at[0], 1 - at[1], mine, other, f)
        for n, (group, k) in enumerate(PLACES):
            rows = slice(n * PART, (n + 1) * PART)
            outs[group][k, f, :, :HALF] = first[rows].astype(bf16)
            outs[group][k, f, :, HALF:] = second[rows].astype(bf16)


def image_own(at, act_factor, grad_factor, mine, other, *outs):
    for f, factor in enumerate((act_factor, grad_factor)):
        first, second = image_rows(factor, at[0], at[1], mine, other, f)
        for k in range(Z):
            rows = slice(k * PART, (k + 1) * PART)
            outs[k][f, :, :HALF] = first[rows]
            outs[k][f, :, HALF:] = second[rows]
        square = sum(jnp.square(part[:, factor_columns(f)].astype(f32)) for part in (mine, other))
        outs[Z][f : f + 1] = jnp.sum(square, axis=0, keepdims=True)


def last_sum(own, away, squares, *refs):
    came, out = refs[:-1], refs[-1]
    total = add_up(own[...] + away[2].astype(f32), [part[...] for part in came])
    out[:, :, :TOKENS] = total.astype(bf16)
    row = lax.broadcasted_iota(jnp.int32, (PART, EXTRA), 0)
    for f in range(2):
        rest = jnp.full((PART, EXTRA), jnp.sum(squares[f : f + 1]))
        parts = jnp.zeros((PART, EXTRA), f32)
        for k in range(3):
            part = rest.astype(bf16).astype(f32)
            parts = jnp.where(row == k, part, parts)
            rest = rest - part
        out[f, :, TOKENS:] = parts.astype(bf16)


def changes(chunks, mine, other, f):
    image = jnp.concatenate([c[f, :, :TOKENS] for c in chunks], axis=0)
    change = dot(image[:, :HALF], mine[:, factor_columns(f)])
    return change + dot(image[:, HALF:], other[:, factor_columns(f)])


def own_changes(mine, other, *refs):
    chunks, (out, squares) = refs[:Z], refs[Z:]
    for f in range(2):
        out[f] = changes(chunks, mine, other, f)
        squares[f : f + 1] = share_sum(chunks, f)


def share_sum(chunks, f):
    return sum(jnp.sum(c[f, :, TOKENS:].astype(f32), axis=0, keepdims=True) for c in chunks)


def update(at, act_factor, grad_factor, mine, other, own_change, squares, *refs):
    chunks, outs = refs[:Z], refs[Z:]
    for f, (factor, out) in enumerate(((act_factor, outs[0]), (grad_factor, outs[1]))):
        total = squares[1 - f : 2 - f] + share_sum(chunks, 1 - f)
        scale = total[:, :1] / (TOKENS * D) * (gram_scale / TOKENS)
        for side in range(YL):
            change = own_change[f] if side == 0 else changes(chunks, mine, other, f)
            half = pl.ds(at[1] if side == 0 else 1 - at[1], 1)
            for k, e in enumerate(GATHER):
                place = (pl.ds(lax.rem(at[0] + (e + Z), Z), 1), half)
                kept = factor[place].reshape(PART, WIDTH).astype(f32)
                new = keep_scale * kept - scale * change[k * PART : (k + 1) * PART]
                out[place] = new.astype(bf16).reshape(1, 1, PART, WIDTH)


def after(a, *others):
    for other in others:
        a = a + jnp.minimum(jnp.abs(other), 0)
    return a


def local(activations, cotangents, act_factor, grad_factor):
    core, z, yl = (lax.axis_index(name) for name in ("core", "z", "yl"))
    product = 4 * HALF * ROWS * WIDTH
    given = (activations, cotangents, act_factor, grad_factor)
    scratch = [pltpu.VMEM((HALF, ROWS), bf16), pltpu.VMEM((ROWS, WIDTH), bf16)] * 2
    scratch.append(pltpu.SemaphoreType.DMA((4,)))
    setup = dict(flops=product, memory=pltpu.HBM, scratch=scratch, room=58)
    (away,) = kernel_call(project, [((HALF, 2 * WIDTH), bf16)], *given, index=[1 - core], **setup)
    came = shift(away, "core", CORE)
    (total,) = kernel_call(project, [((HALF, 2 * WIDTH), f32)], *given, index=[core], **setup)
    total = (total + came.astype(f32)).astype(bf16)
    group = X * YH
    chunks = (group, HALF // group, 2 * WIDTH)
    parts = lax.all_to_all(total.reshape(chunks), ("x", "yh"), 0, 0, tiled=True)
    (copies,) = kernel_call(project_sum, [(chunks, bf16)], parts)
    mine = lax.all_to_all(copies, ("x", "yh"), 0, 0, tiled=True).reshape(HALF, 2 * WIDTH)
    other = shift(mine, "core", CORE)

    factors = [f.reshape(Z, YL, PART, WIDTH) for f in (act_factor, grad_factor)]
    shape = (2, PART, TOKENS)
    sent = [((sum(g == group for g, _ in PLACES),) + shape, bf16) for group in range(3)]
    away = kernel_call(image_away, sent, *factors, mine, other, index=[z, yl], flops=product)
    crossed = [shift(away[0], "yl", YL)]
    crossed.append(shift(after(away[1], crossed[0][0]), "yl", YL))
    *own, squares = kernel_call(
        image_own, [(shape, f32)] * Z + [((2, WIDTH), f32)], *factors, mine, other, index=[z, yl], flops=product
    )
    def partial(n):
        group, k = PLACES[n]
        return own[n] + crossed[group][k].astype(f32)

    relayed = [shift(partial(n).astype(bf16), "z", Z, by) for n, by in ((0, 1), (1, -1))]
    crossed.append(shift(after(away[2], relayed[0]), "yl", YL))
    opposite = add_up(partial(2), relayed).astype(bf16)
    came = [shift(opposite, "z", Z, 4)]
    came += [shift(partial(n).astype(bf16), "z", Z, REDUCE[n]) for n in (3, 4, 5, 6)]
    shape = (2, PART, TOKENS + EXTRA)
    (final,) = kernel_call(last_sum, [(shape, bf16)], own[7], crossed[2], squares, *came)

    opposite = shift(final, "z", Z, 4)
    held = [final] + [shift(final, "z", Z, by) for by in (1, -1)]
    crossed = [shift(a, "yl", YL) for a in held]
    held += [opposite] + [shift(after(final, held[1]), "z", Z, by) for by in (2, -2)]
    opposite = after(opposite, crossed[0], crossed[1])
    held += [shift(opposite, "z", Z, by) for by in (1, -1)]
    crossed += [shift(a, "yl", YL) for a in held[3:]]
    changed, squares = kernel_call(
        own_changes, [((2, ROWS // YL, WIDTH), f32), ((2, EXTRA), f32)], mine, other, *held, flops=product
    )
    outs = kernel_call(
        update, [((Z, YL, PART, WIDTH), bf16)] * 2, *factors, mine, other, changed, squares, *crossed, index=[z, yl], flops=product
    )
    return tuple(out.reshape(ROWS, WIDTH) for out in outs)


def solution(mesh):
    fine = Mesh(mesh.devices.reshape(X, YH, CORE, Z, YL), ROW + COL)
    return jax.shard_map(
        local,
        mesh=fine,
        in_specs=(P(None, ROW), P(None, ROW), P(ROW, COL), P(ROW, COL)),
        out_specs=(P(ROW, COL), P(ROW, COL)),
        check_vma=False,
    )
```

```python
import jax
import jax.numpy as jnp
from jax import lax
from jax.experimental import pallas as pl
from jax.experimental.pallas import tpu as pltpu
from jax.sharding import Mesh, PartitionSpec as P

D = 8192
TOKENS = 1024
X, YH, CORE, Z, YL = 4, 2, 2, 8, 2
ROW = ("x", "yh", "core")
COL = ("z", "yl")
ROWS = D // (X * YH * CORE)
WIDTH = D // (Z * YL)
HALF = TOKENS // CORE
EXTRA = 128
PART = ROWS // (Z * YL)

REDUCE = (4, -3, 3, -2, 2, -1, 1, 0)
PLACES = ((0, 0), (1, 0), (1, 1), (2, 0), (2, 1), (3, 0), (3, 1), (4, 0))
GATHER = (0, -1, 1, -2, 2, -3, 3, -4)

keep_scale = 1.45
gram_scale = 0.5

f32 = jnp.float32
bf16 = jnp.bfloat16


def dot(a, b):
    return jnp.dot(a, b, preferred_element_type=f32)


def dot_t(a, b):
    return lax.dot_general(a, b, (((1,), (1,)), ((), ())), preferred_element_type=f32)


def shift(a, axis, size, by=1):
    return lax.ppermute(a, axis, [(i, (i + by) % size) for i in range(size)])


def kernel_call(body, outs, *args, index=None, flops=0, memory=pltpu.VMEM, scratch=(), room=48):
    specs = [pl.BlockSpec(memory_space=memory)] * len(args)
    if index is not None:
        specs = [pl.BlockSpec(memory_space=pltpu.SMEM)] + specs
        args = (jnp.stack([i.astype(jnp.int32) for i in index]),) + args
    size = sum(a.size * a.dtype.itemsize for a in args)
    return pl.pallas_call(
        body,
        out_shape=[jax.ShapeDtypeStruct(shape, dtype) for shape, dtype in outs],
        in_specs=specs,
        out_specs=[pl.BlockSpec(memory_space=pltpu.VMEM)] * len(outs),
        scratch_shapes=scratch,
        compiler_params=pltpu.CompilerParams(vmem_limit_bytes=room * 2**20),
        cost_estimate=pl.CostEstimate(flops=flops, bytes_accessed=size, transcendentals=0),
    )(*args)


def projected(which, given, bufs, sems):
    rows = pl.ds(pl.multiple_of(which[0] * HALF, HALF), HALF)
    refs = (given[0].at[rows], given[2], given[1].at[rows], given[3])
    copies = [pltpu.make_async_copy(r, buf, sems.at[i]) for i, (r, buf) in enumerate(zip(refs, bufs))]
    for copy in copies:
        copy.start()
    for f in range(2):
        copies[2 * f].wait()
        copies[2 * f + 1].wait()
        yield f, dot(bufs[2 * f][...], bufs[2 * f + 1][...])


def project(which, acts, cots, act_factor, grad_factor, out, *scratch):
    for f, total in projected(which, (acts, cots, act_factor, grad_factor), scratch[:4], scratch[4]):
        out[:, factor_columns(f)] = total.astype(out.dtype)


def project_own(which, acts, cots, act_factor, grad_factor, came, out):
    rows = pl.ds(pl.multiple_of(which[0] * HALF, HALF), HALF)
    for f, (part, factor) in enumerate(((acts, act_factor), (cots, grad_factor))):
        cols = factor_columns(f)
        out[:, cols] = (dot(part[rows, :], factor[...]) + came[:, cols].astype(f32)).astype(bf16)


def project_sum(parts, copies):
    total = parts[0].astype(f32)
    for k in range(1, X * YH):
        total = total + parts[k].astype(f32)
    own = total.astype(bf16)
    for k in range(X * YH):
        copies[k] = own


def factor_columns(f):
    return slice(f * WIDTH, (f + 1) * WIDTH)


def image_rows(factor, z, side, mine, other, f, chunks):
    rows = [factor[pl.ds(lax.rem(z + (e + Z), Z), 1), pl.ds(side, 1)].reshape(PART, WIDTH) for e in chunks]
    rows = jnp.concatenate(rows, axis=0)
    return (
        dot_t(rows, mine[:, factor_columns(f)]),
        dot_t(rows, other[:, factor_columns(f)]),
    )


def image_first(at, act_factor, grad_factor, mine, other, out):
    for f, factor in enumerate((act_factor, grad_factor)):
        first, second = image_rows(factor, at[0], 1 - at[1], mine, other, f, REDUCE[:1])
        out[0, f, :, :HALF] = first.astype(bf16)
        out[0, f, :, HALF:] = second.astype(bf16)


def image_away(at, act_factor, grad_factor, mine, other, *outs):
    for f, factor in enumerate((act_factor, grad_factor)):
        first, second = image_rows(factor, at[0], 1 - at[1], mine, other, f, REDUCE[1:])
        for n, (group, k) in enumerate(PLACES[1:]):
            rows = slice(n * PART, (n + 1) * PART)
            outs[group - 1][k, f, :, :HALF] = first[rows].astype(bf16)
            outs[group - 1][k, f, :, HALF:] = second[rows].astype(bf16)


def image_own(at, act_factor, grad_factor, mine, other, *outs):
    for f, factor in enumerate((act_factor, grad_factor)):
        first, second = image_rows(factor, at[0], at[1], mine, other, f, REDUCE)
        for k in range(Z):
            rows = slice(k * PART, (k + 1) * PART)
            outs[k][f, :, :HALF] = first[rows]
            outs[k][f, :, HALF:] = second[rows]
        square = sum(jnp.square(part[:, factor_columns(f)].astype(f32)) for part in (mine, other))
        outs[Z][f : f + 1] = jnp.sum(square, axis=0, keepdims=True)


def last_sum(own, away, up, down, squares, out):
    total = own[...] + away[0].astype(f32) + up[...].astype(f32) + down[...].astype(f32)
    out[:, :, :TOKENS] = total.astype(bf16)
    row = lax.broadcasted_iota(jnp.int32, (PART, EXTRA), 0)
    for f in range(2):
        rest = jnp.full((PART, EXTRA), jnp.sum(squares[f : f + 1]))
        parts = jnp.zeros((PART, EXTRA), f32)
        for k in range(3):
            part = rest.astype(bf16).astype(f32)
            parts = jnp.where(row == k, part, parts)
            rest = rest - part
        out[f, :, TOKENS:] = parts.astype(bf16)


def changes(chunks, mine, other, f):
    image = jnp.concatenate([c[f, :, :TOKENS] for c in chunks], axis=0)
    change = dot(image[:, :HALF], mine[:, factor_columns(f)])
    return change + dot(image[:, HALF:], other[:, factor_columns(f)])


def own_changes(mine, other, *refs):
    chunks, (out, squares) = refs[:Z], refs[Z:]
    for f in range(2):
        out[f] = changes(chunks, mine, other, f)
        squares[f : f + 1] = share_sum(chunks, f)


def share_sum(chunks, f):
    return sum(jnp.sum(c[f, :, TOKENS:].astype(f32), axis=0, keepdims=True) for c in chunks)


def update(at, act_factor, grad_factor, mine, other, own_change, squares, *refs):
    chunks, outs = refs[:Z], refs[Z:]
    for f, (factor, out) in enumerate(((act_factor, outs[0]), (grad_factor, outs[1]))):
        total = squares[1 - f : 2 - f] + share_sum(chunks, 1 - f)
        scale = total[:, :1] / (TOKENS * D) * (gram_scale / TOKENS)
        for side in range(YL):
            change = own_change[f] if side == 0 else changes(chunks, mine, other, f)
            half = pl.ds(at[1] if side == 0 else 1 - at[1], 1)
            for k, e in enumerate(GATHER):
                place = (pl.ds(lax.rem(at[0] + (e + Z), Z), 1), half)
                kept = factor[place].reshape(PART, WIDTH).astype(f32)
                new = keep_scale * kept - scale * change[k * PART : (k + 1) * PART]
                out[place] = new.astype(bf16).reshape(1, 1, PART, WIDTH)


def after(a, *others):
    for other in others:
        a = a + jnp.minimum(jnp.abs(other), 0)
    return a


def local(activations, cotangents, act_factor, grad_factor):
    core, z, yl = (lax.axis_index(name) for name in ("core", "z", "yl"))
    product = 4 * HALF * ROWS * WIDTH
    given = (activations, cotangents, act_factor, grad_factor)
    scratch = [pltpu.VMEM((HALF, ROWS), bf16), pltpu.VMEM((ROWS, WIDTH), bf16)] * 2
    scratch.append(pltpu.SemaphoreType.DMA((4,)))
    setup = dict(flops=product, memory=pltpu.HBM, scratch=scratch, room=58)
    (away,) = kernel_call(project, [((HALF, 2 * WIDTH), bf16)], *given, index=[1 - core], **setup)
    came = shift(away, "core", CORE)
    (total,) = kernel_call(project_own, [((HALF, 2 * WIDTH), bf16)], *given, came, index=[core], flops=product)
    group = X * YH
    chunks = (group, HALF // group, 2 * WIDTH)
    parts = lax.all_to_all(total.reshape(chunks), ("x", "yh"), 0, 0, tiled=True)
    (copies,) = kernel_call(project_sum, [(chunks, bf16)], parts)
    mine = lax.all_to_all(copies, ("x", "yh"), 0, 0, tiled=True).reshape(HALF, 2 * WIDTH)
    other = shift(mine, "core", CORE)

    factors = [f.reshape(Z, YL, PART, WIDTH) for f in (act_factor, grad_factor)]
    shape = (2, PART, TOKENS)
    sent = [((sum(g == group for g, _ in PLACES),) + shape, bf16) for group in range(5)]
    first = kernel_call(image_first, sent[:1], *factors, mine, other, index=[z, yl], flops=product // Z)
    away = first + kernel_call(image_away, sent[1:], *factors, mine, other, index=[z, yl], flops=product)
    away = [shift(a, "yl", YL) for a in away]
    *own, squares = kernel_call(
        image_own, [(shape, f32)] * Z + [((2, WIDTH), f32)], *factors, mine, other, index=[z, yl], flops=product
    )
    up = own[0] + away[0][0].astype(f32)
    down = own[1] + away[1][0].astype(f32)
    for step in (1, 2, 3):
        up = shift(up.astype(bf16), "z", Z, 1)
        up = own[2 * step] + away[step][1].astype(f32) + up.astype(f32)
        down = shift(down.astype(bf16), "z", Z, -1)
        if step < 3:
            down = own[2 * step + 1] + away[step + 1][0].astype(f32) + down.astype(f32)
    up = shift(up.astype(bf16), "z", Z, 1)
    shape = (2, PART, TOKENS + EXTRA)
    (up,) = kernel_call(last_sum, [(shape, bf16)], own[7], away[4], up, down, squares)

    down = up
    held, crossed = [up], [shift(up, "yl", YL)]
    for step in (1, 2, 3):
        if step == 3:
            up, down = after(up, crossed[0]), after(down, crossed[0])
        up, down = shift(up, "z", Z, 1), shift(down, "z", Z, -1)
        held += [up, down]
        crossed += [shift(up, "yl", YL), shift(down, "yl", YL)]
    up = shift(after(up, crossed[1], crossed[2], crossed[3]), "z", Z, 1)
    held.append(up)
    crossed.append(shift(up, "yl", YL))
    changed, squares = kernel_call(
        own_changes, [((2, ROWS // YL, WIDTH), f32), ((2, EXTRA), f32)], mine, other, *held, flops=product
    )
    outs = kernel_call(
        update, [((Z, YL, PART, WIDTH), bf16)] * 2, *factors, mine, other, changed, squares, *crossed, index=[z, yl], flops=product
    )
    return tuple(out.reshape(ROWS, WIDTH) for out in outs)


def solution(mesh):
    fine = Mesh(mesh.devices.reshape(X, YH, CORE, Z, YL), ROW + COL)
    return jax.shard_map(
        local,
        mesh=fine,
        in_specs=(P(None, ROW), P(None, ROW), P(ROW, COL), P(ROW, COL)),
        out_specs=(P(ROW, COL), P(ROW, COL)),
        check_vma=False,
    )
```

```python
import jax
import jax.numpy as jnp
from jax import lax
from jax.experimental import pallas as pl
from jax.experimental.pallas import tpu as pltpu
from jax.sharding import Mesh, PartitionSpec as P

D = 8192
TOKENS = 1024
X, YH, CORE, Z, YL = 4, 2, 2, 8, 2
ROW = ("x", "yh", "core")
COL = ("z", "yl")
ROWS = D // (X * YH * CORE)
WIDTH = D // (Z * YL)
HALF = TOKENS // CORE
EXTRA = 16
LANES = 128
BLOCKS = TOKENS // LANES
PART = ROWS // (Z * YL)

REDUCE = (4, -3, 3, -2, 2, -1, 1, 0)
PLACES = ((0, 0), (1, 0), (1, 1), (2, 0), (2, 1), (3, 0), (3, 1), (4, 0))
GATHER = (0, -1, 1, -2, 2, -3, 3, -4)

keep_scale = 1.45
gram_scale = 0.5

f32 = jnp.float32
bf16 = jnp.bfloat16


def dot(a, b):
    return jnp.dot(a, b, preferred_element_type=f32)


def dot_t(a, b):
    return lax.dot_general(a, b, (((1,), (1,)), ((), ())), preferred_element_type=f32)


def shift(a, axis, size, by=1):
    return lax.ppermute(a, axis, [(i, (i + by) % size) for i in range(size)])


def kernel_call(body, outs, *args, index=None, flops=0, memory=pltpu.VMEM, scratch=(), room=48):
    specs = [pl.BlockSpec(memory_space=memory)] * len(args)
    if index is not None:
        specs = [pl.BlockSpec(memory_space=pltpu.SMEM)] + specs
        args = (jnp.stack([i.astype(jnp.int32) for i in index]),) + args
    size = sum(a.size * a.dtype.itemsize for a in args)
    return pl.pallas_call(
        body,
        out_shape=[jax.ShapeDtypeStruct(shape, dtype) for shape, dtype in outs],
        in_specs=specs,
        out_specs=[pl.BlockSpec(memory_space=pltpu.VMEM)] * len(outs),
        scratch_shapes=scratch,
        compiler_params=pltpu.CompilerParams(vmem_limit_bytes=room * 2**20),
        cost_estimate=pl.CostEstimate(flops=flops, bytes_accessed=size, transcendentals=0),
    )(*args)


def projected(which, given, bufs, sems):
    rows = pl.ds(pl.multiple_of(which[0] * HALF, HALF), HALF)
    refs = (given[0].at[rows], given[2], given[1].at[rows], given[3])
    copies = [pltpu.make_async_copy(r, buf, sems.at[i]) for i, (r, buf) in enumerate(zip(refs, bufs))]
    for copy in copies:
        copy.start()
    for f in range(2):
        copies[2 * f].wait()
        copies[2 * f + 1].wait()
        yield f, dot(bufs[2 * f][...], bufs[2 * f + 1][...])


def project(which, acts, cots, act_factor, grad_factor, out, *scratch):
    for f, total in projected(which, (acts, cots, act_factor, grad_factor), scratch[:4], scratch[4]):
        out[:, factor_columns(f)] = total.astype(out.dtype)


def project_own(which, acts, cots, act_factor, grad_factor, came, out):
    rows = pl.ds(pl.multiple_of(which[0] * HALF, HALF), HALF)
    for f, (part, factor) in enumerate(((acts, act_factor), (cots, grad_factor))):
        cols = factor_columns(f)
        out[:, cols] = (dot(part[rows, :], factor[...]) + came[:, cols].astype(f32)).astype(bf16)


def project_sum(parts, copies):
    total = parts[0].astype(f32)
    for k in range(1, X * YH):
        total = total + parts[k].astype(f32)
    own = total.astype(bf16)
    for k in range(X * YH):
        copies[k] = own


def factor_columns(f):
    return slice(f * WIDTH, (f + 1) * WIDTH)


def image_rows(factor, z, side, mine, other, f, chunks):
    rows = [factor[pl.ds(lax.rem(z + (e + Z), Z), 1), pl.ds(side, 1)].reshape(PART, WIDTH) for e in chunks]
    rows = jnp.concatenate(rows, axis=0)
    return (
        dot_t(rows, mine[:, factor_columns(f)]),
        dot_t(rows, other[:, factor_columns(f)]),
    )


def image_first(at, act_factor, grad_factor, mine, other, out):
    for f, factor in enumerate((act_factor, grad_factor)):
        first, second = image_rows(factor, at[0], 1 - at[1], mine, other, f, REDUCE[:1])
        out[0, f, :, :HALF] = first.astype(bf16)
        out[0, f, :, HALF:] = second.astype(bf16)


def image_away(at, act_factor, grad_factor, mine, other, *outs):
    for f, factor in enumerate((act_factor, grad_factor)):
        first, second = image_rows(factor, at[0], 1 - at[1], mine, other, f, REDUCE[1:])
        for n, (group, k) in enumerate(PLACES[1:]):
            rows = slice(n * PART, (n + 1) * PART)
            outs[group - 1][k, f, :, :HALF] = first[rows].astype(bf16)
            outs[group - 1][k, f, :, HALF:] = second[rows].astype(bf16)


def image_own(at, act_factor, grad_factor, mine, other, *outs):
    for f, factor in enumerate((act_factor, grad_factor)):
        first, second = image_rows(factor, at[0], at[1], mine, other, f, REDUCE)
        for k in range(Z):
            rows = slice(k * PART, (k + 1) * PART)
            outs[k][f, :, :HALF] = first[rows]
            outs[k][f, :, HALF:] = second[rows]
        square = sum(jnp.square(part[:, factor_columns(f)].astype(f32)) for part in (mine, other))
        outs[Z][f : f + 1] = jnp.sum(square, axis=0, keepdims=True)


def last_sum(own, away, up, down, squares, out):
    total = own[...] + away[0].astype(f32) + up[...].astype(f32) + down[...].astype(f32)
    total = total.astype(bf16)
    for n in range(2 * BLOCKS):
        f, block = divmod(n, BLOCKS)
        out[n * PART : (n + 1) * PART, :] = total[f, :, block * LANES : (block + 1) * LANES]
    row = lax.broadcasted_iota(jnp.int32, (EXTRA, LANES), 0)
    parts = jnp.zeros((EXTRA, LANES), f32)
    for f in range(2):
        rest = jnp.full((EXTRA, LANES), jnp.sum(squares[f : f + 1]))
        for k in range(3):
            part = rest.astype(bf16).astype(f32)
            parts = jnp.where(row == f * EXTRA // 2 + k, part, parts)
            rest = rest - part
    out[2 * BLOCKS * PART :, :] = parts.astype(bf16)


def changes(chunks, mine, other, f):
    def image(c):
        first = f * BLOCKS
        return jnp.concatenate([c[n * PART : (n + 1) * PART, :] for n in range(first, first + BLOCKS)], axis=1)

    image = jnp.concatenate([image(c) for c in chunks], axis=0)
    change = dot(image[:, :HALF], mine[:, factor_columns(f)])
    return change + dot(image[:, HALF:], other[:, factor_columns(f)])


def own_changes(mine, other, *refs):
    chunks, (out, squares) = refs[:Z], refs[Z:]
    for f in range(2):
        out[f] = changes(chunks, mine, other, f)
        squares[f : f + 1] = share_sum(chunks, f)


def share_sum(chunks, f):
    shares = sum(c[2 * BLOCKS * PART :, :].astype(f32) for c in chunks)
    half = EXTRA // 2
    return jnp.sum(shares[f * half : (f + 1) * half], axis=0, keepdims=True)


def update(at, act_factor, grad_factor, mine, other, own_change, squares, *refs):
    chunks, outs = refs[:Z], refs[Z:]
    for f, (factor, out) in enumerate(((act_factor, outs[0]), (grad_factor, outs[1]))):
        total = squares[1 - f : 2 - f] + share_sum(chunks, 1 - f)
        scale = total[:, :1] / (TOKENS * D) * (gram_scale / TOKENS)
        for side in range(YL):
            change = own_change[f] if side == 0 else changes(chunks, mine, other, f)
            half = pl.ds(at[1] if side == 0 else 1 - at[1], 1)
            for k, e in enumerate(GATHER):
                place = (pl.ds(lax.rem(at[0] + (e + Z), Z), 1), half)
                kept = factor[place].reshape(PART, WIDTH).astype(f32)
                new = keep_scale * kept - scale * change[k * PART : (k + 1) * PART]
                out[place] = new.astype(bf16).reshape(1, 1, PART, WIDTH)


def after(a, *others):
    for other in others:
        a = a + jnp.minimum(jnp.abs(other), 0)
    return a


def local(activations, cotangents, act_factor, grad_factor):
    core, z, yl = (lax.axis_index(name) for name in ("core", "z", "yl"))
    product = 4 * HALF * ROWS * WIDTH
    given = (activations, cotangents, act_factor, grad_factor)
    scratch = [pltpu.VMEM((HALF, ROWS), bf16), pltpu.VMEM((ROWS, WIDTH), bf16)] * 2
    scratch.append(pltpu.SemaphoreType.DMA((4,)))
    setup = dict(flops=product, memory=pltpu.HBM, scratch=scratch, room=58)
    (away,) = kernel_call(project, [((HALF, 2 * WIDTH), bf16)], *given, index=[1 - core], **setup)
    came = shift(away, "core", CORE)
    (total,) = kernel_call(project_own, [((HALF, 2 * WIDTH), bf16)], *given, came, index=[core], flops=product)
    group = X * YH
    chunks = (group, HALF // group, 2 * WIDTH)
    parts = lax.all_to_all(total.reshape(chunks), ("x", "yh"), 0, 0, tiled=True)
    (copies,) = kernel_call(project_sum, [(chunks, bf16)], parts)
    mine = lax.all_to_all(copies, ("x", "yh"), 0, 0, tiled=True).reshape(HALF, 2 * WIDTH)
    other = shift(mine, "core", CORE)

    factors = [f.reshape(Z, YL, PART, WIDTH) for f in (act_factor, grad_factor)]
    shape = (2, PART, TOKENS)
    sent = [((sum(g == group for g, _ in PLACES),) + shape, bf16) for group in range(5)]
    first = kernel_call(image_first, sent[:1], *factors, mine, other, index=[z, yl], flops=product // Z)
    away = first + kernel_call(image_away, sent[1:], *factors, mine, other, index=[z, yl], flops=product)
    away = [shift(a, "yl", YL) for a in away]
    *own, squares = kernel_call(
        image_own, [(shape, f32)] * Z + [((2, WIDTH), f32)], *factors, mine, other, index=[z, yl], flops=product
    )
    up = own[0] + away[0][0].astype(f32)
    down = own[1] + away[1][0].astype(f32)
    for step in (1, 2, 3):
        up = shift(up.astype(bf16), "z", Z, 1)
        up = own[2 * step] + away[step][1].astype(f32) + up.astype(f32)
        down = shift(down.astype(bf16), "z", Z, -1)
        if step < 3:
            down = own[2 * step + 1] + away[step + 1][0].astype(f32) + down.astype(f32)
    up = shift(up.astype(bf16), "z", Z, 1)
    shape = (2 * BLOCKS * PART + EXTRA, LANES)
    (up,) = kernel_call(last_sum, [(shape, bf16)], own[7], away[4], up, down, squares)

    down = up
    held, crossed = [up], [shift(up, "yl", YL)]
    for step in (1, 2, 3):
        if step == 3:
            up, down = after(up, crossed[0]), after(down, crossed[0])
        up, down = shift(up, "z", Z, 1), shift(down, "z", Z, -1)
        held += [up, down]
        crossed += [shift(up, "yl", YL), shift(down, "yl", YL)]
    up = shift(after(up, *crossed[1:5]), "z", Z, 1)
    held.append(up)
    crossed.append(shift(up, "yl", YL))
    changed, squares = kernel_call(
        own_changes, [((2, ROWS // YL, WIDTH), f32), ((2, LANES), f32)], mine, other, *held, flops=product
    )
    outs = kernel_call(
        update, [((Z, YL, PART, WIDTH), bf16)] * 2, *factors, mine, other, changed, squares, *crossed, index=[z, yl], flops=product
    )
    return tuple(out.reshape(ROWS, WIDTH) for out in outs)


def solution(mesh):
    fine = Mesh(mesh.devices.reshape(X, YH, CORE, Z, YL), ROW + COL)
    return jax.shard_map(
        local,
        mesh=fine,
        in_specs=(P(None, ROW), P(None, ROW), P(ROW, COL), P(ROW, COL)),
        out_specs=(P(ROW, COL), P(ROW, COL)),
        check_vma=False,
    )
```

```python
import functools

import jax
import jax.numpy as jnp
from jax import lax
from jax.experimental import pallas as pl
from jax.experimental.pallas import tpu as pltpu
from jax.sharding import Mesh, PartitionSpec as P

D = 8192
TOKENS = 1024
X, YH, CORE, Z, YL = 4, 2, 2, 8, 2
ROW = ("x", "yh", "core")
COL = ("z", "yl")
ROWS = D // (X * YH * CORE)
WIDTH = D // (Z * YL)
HALF = TOKENS // CORE
EXTRA = 16
LANES = 128
BLOCKS = TOKENS // LANES
PART = ROWS // (Z * YL)

REDUCE = (4, -3, 3, -2, 2, -1, 1, 0)
FIRST = 3
GATHER = (0, -1, 1, -2, 2, -3, 3, -4)

keep_scale = 1.45
gram_scale = 0.5

f32 = jnp.float32
bf16 = jnp.bfloat16


def dot(a, b):
    return jnp.dot(a, b, preferred_element_type=f32)


def dot_t(a, b):
    return lax.dot_general(a, b, (((1,), (1,)), ((), ())), preferred_element_type=f32)


def shift(a, axis, size, by=1):
    return lax.ppermute(a, axis, [(i, (i + by) % size) for i in range(size)])


def kernel_call(body, outs, *args, index=None, flops=0, memory=pltpu.VMEM, scratch=(), room=48):
    specs = [pl.BlockSpec(memory_space=memory)] * len(args)
    if index is not None:
        specs = [pl.BlockSpec(memory_space=pltpu.SMEM)] + specs
        args = (jnp.stack([i.astype(jnp.int32) for i in index]),) + args
    size = sum(a.size * a.dtype.itemsize for a in args)
    return pl.pallas_call(
        body,
        out_shape=[jax.ShapeDtypeStruct(shape, dtype) for shape, dtype in outs],
        in_specs=specs,
        out_specs=[pl.BlockSpec(memory_space=pltpu.VMEM)] * len(outs),
        scratch_shapes=scratch,
        compiler_params=pltpu.CompilerParams(vmem_limit_bytes=room * 2**20),
        cost_estimate=pl.CostEstimate(flops=flops, bytes_accessed=size, transcendentals=0),
    )(*args)


def projected(which, given, bufs, sems):
    rows = pl.ds(pl.multiple_of(which[0] * HALF, HALF), HALF)
    refs = (given[0].at[rows], given[2], given[1].at[rows], given[3])
    copies = [pltpu.make_async_copy(r, buf, sems.at[i]) for i, (r, buf) in enumerate(zip(refs, bufs))]
    for copy in copies:
        copy.start()
    for f in range(2):
        copies[2 * f].wait()
        copies[2 * f + 1].wait()
        yield f, dot(bufs[2 * f][...], bufs[2 * f + 1][...])


def project(which, acts, cots, act_factor, grad_factor, out, *scratch):
    for f, total in projected(which, (acts, cots, act_factor, grad_factor), scratch[:4], scratch[4]):
        out[:, factor_columns(f)] = total.astype(out.dtype)


def project_own(which, acts, cots, act_factor, grad_factor, came, out):
    rows = pl.ds(pl.multiple_of(which[0] * HALF, HALF), HALF)
    for f, (part, factor) in enumerate(((acts, act_factor), (cots, grad_factor))):
        cols = factor_columns(f)
        out[:, cols] = (dot(part[rows, :], factor[...]) + came[:, cols].astype(f32)).astype(bf16)


def project_sum(parts, copies):
    total = parts[0].astype(f32)
    for k in range(1, X * YH):
        total = total + parts[k].astype(f32)
    own = total.astype(bf16)
    for k in range(X * YH):
        copies[k] = own


def factor_columns(f):
    return slice(f * WIDTH, (f + 1) * WIDTH)


def image_rows(factor, z, side, chunks):
    rows = [factor[pl.ds(lax.rem(z + (e + Z), Z), 1), pl.ds(side, 1)].reshape(PART, WIDTH) for e in chunks]
    return jnp.concatenate(rows, axis=0)


def image_first(at, act_factor, grad_factor, part, out):
    for f, factor in enumerate((act_factor, grad_factor)):
        rows = image_rows(factor, at[0], 1 - at[1], REDUCE[:FIRST])
        image = dot_t(rows, part[:, factor_columns(f)]).astype(bf16)
        out[:, f] = image.reshape(FIRST, PART, HALF)


def image_away(at, act_factor, grad_factor, mine, other, *outs):
    for f, factor in enumerate((act_factor, grad_factor)):
        rows = image_rows(factor, at[0], 1 - at[1], REDUCE[FIRST:])
        for part, cols in ((mine, slice(0, HALF)), (other, slice(HALF, TOKENS))):
            image = dot_t(rows, part[:, factor_columns(f)]).astype(bf16)
            for n in range(Z - FIRST):
                outs[n // 2][n % 2, f, :, cols] = image[n * PART : (n + 1) * PART]


def image_own(at, act_factor, grad_factor, mine, other, *outs):
    for f, factor in enumerate((act_factor, grad_factor)):
        rows = image_rows(factor, at[0], at[1], REDUCE)
        for part, cols in ((mine, slice(0, HALF)), (other, slice(HALF, TOKENS))):
            image = dot_t(rows, part[:, factor_columns(f)])
            for k in range(Z):
                outs[k][f, :, cols] = image[k * PART : (k + 1) * PART]
        square = sum(jnp.square(part[:, factor_columns(f)].astype(f32)) for part in (mine, other))
        outs[Z][f : f + 1] = jnp.sum(square, axis=0, keepdims=True)


def joined(n, own, away_mine, away_other, *refs):
    came, out = refs[:-1], refs[-1]
    for away, cols in ((away_mine, slice(0, HALF)), (away_other, slice(HALF, TOKENS))):
        total = own[:, :, cols] + away[n].astype(f32)
        for part in came:
            total = total + part[:, :, cols].astype(f32)
        out[:, :, cols] = total.astype(bf16)


def last_sum(own, away, up, down, squares, out):
    total = own[...] + away[0].astype(f32) + up[...].astype(f32) + down[...].astype(f32)
    total = total.astype(bf16)
    for n in range(2 * BLOCKS):
        f, block = divmod(n, BLOCKS)
        out[n * PART : (n + 1) * PART, :] = total[f, :, block * LANES : (block + 1) * LANES]
    row = lax.broadcasted_iota(jnp.int32, (EXTRA, LANES), 0)
    parts = jnp.zeros((EXTRA, LANES), f32)
    for f in range(2):
        rest = jnp.full((EXTRA, LANES), jnp.sum(squares[f : f + 1]))
        for k in range(3):
            part = rest.astype(bf16).astype(f32)
            parts = jnp.where(row == f * EXTRA // 2 + k, part, parts)
            rest = rest - part
    out[2 * BLOCKS * PART :, :] = parts.astype(bf16)


def changes(chunks, mine, other, f):
    def image(c):
        first = f * BLOCKS
        return jnp.concatenate([c[n * PART : (n + 1) * PART, :] for n in range(first, first + BLOCKS)], axis=1)

    image = jnp.concatenate([image(c) for c in chunks], axis=0)
    change = dot(image[:, :HALF], mine[:, factor_columns(f)])
    return change + dot(image[:, HALF:], other[:, factor_columns(f)])


def own_changes(mine, other, *refs):
    chunks, (out, squares) = refs[:Z], refs[Z:]
    for f in range(2):
        out[f] = changes(chunks, mine, other, f)
        squares[f : f + 1] = share_sum(chunks, f)


def share_sum(chunks, f):
    shares = sum(c[2 * BLOCKS * PART :, :].astype(f32) for c in chunks)
    half = EXTRA // 2
    return jnp.sum(shares[f * half : (f + 1) * half], axis=0, keepdims=True)


def update(at, act_factor, grad_factor, mine, other, own_change, squares, *refs):
    chunks, outs = refs[:Z], refs[Z:]
    for f, (factor, out) in enumerate(((act_factor, outs[0]), (grad_factor, outs[1]))):
        total = squares[1 - f : 2 - f] + share_sum(chunks, 1 - f)
        scale = total[:, :1] / (TOKENS * D) * (gram_scale / TOKENS)
        for side in range(YL):
            change = own_change[f] if side == 0 else changes(chunks, mine, other, f)
            half = pl.ds(at[1] if side == 0 else 1 - at[1], 1)
            for k, e in enumerate(GATHER):
                place = (pl.ds(lax.rem(at[0] + (e + Z), Z), 1), half)
                kept = factor[place].reshape(PART, WIDTH).astype(f32)
                new = keep_scale * kept - scale * change[k * PART : (k + 1) * PART]
                out[place] = new.astype(bf16).reshape(1, 1, PART, WIDTH)


def after(a, *others):
    for other in others:
        a = a + jnp.minimum(jnp.abs(other), 0)
    return a


def local(activations, cotangents, act_factor, grad_factor):
    core, z, yl = (lax.axis_index(name) for name in ("core", "z", "yl"))
    product = 4 * HALF * ROWS * WIDTH
    given = (activations, cotangents, act_factor, grad_factor)
    scratch = [pltpu.VMEM((HALF, ROWS), bf16), pltpu.VMEM((ROWS, WIDTH), bf16)] * 2
    scratch.append(pltpu.SemaphoreType.DMA((4,)))
    setup = dict(flops=product, memory=pltpu.HBM, scratch=scratch, room=58)
    (away,) = kernel_call(project, [((HALF, 2 * WIDTH), bf16)], *given, index=[1 - core], **setup)
    came = shift(away, "core", CORE)
    (total,) = kernel_call(project_own, [((HALF, 2 * WIDTH), bf16)], *given, came, index=[core], flops=product)
    group = X * YH
    chunks = (group, HALF // group, 2 * WIDTH)
    parts = lax.all_to_all(total.reshape(chunks), ("x", "yh"), 0, 0, tiled=True)
    (copies,) = kernel_call(project_sum, [(chunks, bf16)], parts)
    mine = lax.all_to_all(copies, ("x", "yh"), 0, 0, tiled=True).reshape(HALF, 2 * WIDTH)
    other = shift(mine, "core", CORE)

    factors = [f.reshape(Z, YL, PART, WIDTH) for f in (act_factor, grad_factor)]
    shape = (2, PART, TOKENS)
    at, work = [z, yl], product // 4
    first = [((FIRST, 2, PART, HALF), bf16)]
    (away_mine,) = kernel_call(image_first, first, *factors, mine, index=at, flops=work)
    away_mine = shift(away_mine, "yl", YL)
    (away_other,) = kernel_call(image_first, first, *factors, other, index=at, flops=work)
    away_other = shift(away_other, "yl", YL)
    sent = [((count,) + shape, bf16) for count in (2, 2, 1)]
    away = kernel_call(image_away, sent, *factors, mine, other, index=at, flops=product)
    away = [shift(a, "yl", YL) for a in away]
    *own, squares = kernel_call(
        image_own, [(shape, f32)] * Z + [((2, WIDTH), f32)], *factors, mine, other, index=at, flops=product
    )

    def join(n, *came):
        body = functools.partial(joined, n)
        return kernel_call(body, [(shape, bf16)], own[n], away_mine, away_other, *came)[0]

    def add(n, came):
        group, k = divmod(n - FIRST, 2)
        return (own[n] + away[group][k].astype(f32) + came.astype(f32)).astype(bf16)

    up, down = shift(join(0), "z", Z, 1), shift(join(1), "z", Z, -1)
    up, down = shift(join(2, up), "z", Z, 1), shift(add(3, down), "z", Z, -1)
    up, down = shift(add(4, up), "z", Z, 1), shift(add(5, down), "z", Z, -1)
    up = shift(add(6, up), "z", Z, 1)
    shape = (2 * BLOCKS * PART + EXTRA, LANES)
    (up,) = kernel_call(last_sum, [(shape, bf16)], own[7], away[2], up, down, squares)

    down = up
    held, crossed = [up], [shift(up, "yl", YL)]
    for step in (1, 2, 3):
        if step == 3:
            up, down = after(up, crossed[0]), after(down, crossed[0])
        up, down = shift(up, "z", Z, 1), shift(down, "z", Z, -1)
        held += [up, down]
        crossed += [shift(up, "yl", YL), shift(down, "yl", YL)]
    up = shift(after(up, *crossed[1:4]), "z", Z, 1)
    held.append(up)
    crossed.append(shift(up, "yl", YL))
    changed, squares = kernel_call(
        own_changes, [((2, ROWS // YL, WIDTH), f32), ((2, LANES), f32)], mine, other, *held, flops=product
    )
    outs = kernel_call(
        update, [((Z, YL, PART, WIDTH), bf16)] * 2, *factors, mine, other, changed, squares, *crossed, index=[z, yl], flops=product
    )
    return tuple(out.reshape(ROWS, WIDTH) for out in outs)


def solution(mesh):
    fine = Mesh(mesh.devices.reshape(X, YH, CORE, Z, YL), ROW + COL)
    return jax.shard_map(
        local,
        mesh=fine,
        in_specs=(P(None, ROW), P(None, ROW), P(ROW, COL), P(ROW, COL)),
        out_specs=(P(ROW, COL), P(ROW, COL)),
        check_vma=False,
    )
```

```python
import jax
import jax.numpy as jnp
from jax import lax
from jax.experimental import pallas as pl
from jax.experimental.pallas import tpu as pltpu
from jax.sharding import Mesh, PartitionSpec as P

D = 8192
TOKENS = 1024
X, YH, CORE, Z, YL = 4, 2, 2, 8, 2
ROW = ("x", "yh", "core")
COL = ("z", "yl")
ROWS = D // (X * YH * CORE)
WIDTH = D // (Z * YL)
HALF = TOKENS // CORE
EXTRA = 16
LANES = 128
BLOCKS = TOKENS // LANES
PART = ROWS // (Z * YL)

REDUCE = (4, -3, 3, -2, 2, -1, 1, 0)
PLACES = ((0, 0), (1, 0), (1, 1), (2, 0), (2, 1), (3, 0), (3, 1), (4, 0))
GATHER = (0, -1, 1, -2, 2, -3, 3, -4)

keep_scale = 1.45
gram_scale = 0.5

f32 = jnp.float32
bf16 = jnp.bfloat16


def dot(a, b):
    return jnp.dot(a, b, preferred_element_type=f32)


def dot_t(a, b):
    return lax.dot_general(a, b, (((1,), (1,)), ((), ())), preferred_element_type=f32)


def shift(a, axis, size, by=1):
    return lax.ppermute(a, axis, [(i, (i + by) % size) for i in range(size)])


def kernel_call(body, outs, *args, index=None, flops=0, memory=pltpu.VMEM, scratch=(), room=48):
    specs = [pl.BlockSpec(memory_space=memory)] * len(args)
    if index is not None:
        specs = [pl.BlockSpec(memory_space=pltpu.SMEM)] + specs
        args = (jnp.stack([i.astype(jnp.int32) for i in index]),) + args
    size = sum(a.size * a.dtype.itemsize for a in args)
    return pl.pallas_call(
        body,
        out_shape=[jax.ShapeDtypeStruct(shape, dtype) for shape, dtype in outs],
        in_specs=specs,
        out_specs=[pl.BlockSpec(memory_space=pltpu.VMEM)] * len(outs),
        scratch_shapes=scratch,
        compiler_params=pltpu.CompilerParams(vmem_limit_bytes=room * 2**20),
        cost_estimate=pl.CostEstimate(flops=flops, bytes_accessed=size, transcendentals=0),
    )(*args)


def projected(which, given, bufs, sems):
    rows = pl.ds(pl.multiple_of(which[0] * HALF, HALF), HALF)
    refs = (given[0].at[rows], given[2], given[1].at[rows], given[3])
    copies = [pltpu.make_async_copy(r, buf, sems.at[i]) for i, (r, buf) in enumerate(zip(refs, bufs))]
    for copy in copies:
        copy.start()
    for f in range(2):
        copies[2 * f].wait()
        copies[2 * f + 1].wait()
        yield f, dot(bufs[2 * f][...], bufs[2 * f + 1][...])


def project(which, acts, cots, act_factor, grad_factor, out, *scratch):
    for f, total in projected(which, (acts, cots, act_factor, grad_factor), scratch[:4], scratch[4]):
        out[:, factor_columns(f)] = total.astype(out.dtype)


def project_own(which, acts, cots, act_factor, grad_factor, came, out):
    rows = pl.ds(pl.multiple_of(which[0] * HALF, HALF), HALF)
    for f, (part, factor) in enumerate(((acts, act_factor), (cots, grad_factor))):
        cols = factor_columns(f)
        out[:, cols] = (dot(part[rows, :], factor[...]) + came[:, cols].astype(f32)).astype(bf16)


def project_sum(parts, copies):
    total = parts[0].astype(f32)
    for k in range(1, X * YH):
        total = total + parts[k].astype(f32)
    own = total.astype(bf16)
    for k in range(X * YH):
        copies[k] = own


def factor_columns(f):
    return slice(f * WIDTH, (f + 1) * WIDTH)


def image_rows(factor, z, side, mine, other, f, chunks):
    rows = [factor[pl.ds(lax.rem(z + (e + Z), Z), 1), pl.ds(side, 1)].reshape(PART, WIDTH) for e in chunks]
    rows = jnp.concatenate(rows, axis=0)
    return (
        dot_t(rows, mine[:, factor_columns(f)]),
        dot_t(rows, other[:, factor_columns(f)]),
    )


def image_first(at, act_factor, grad_factor, mine, other, out):
    for f, factor in enumerate((act_factor, grad_factor)):
        first, second = image_rows(factor, at[0], 1 - at[1], mine, other, f, REDUCE[:1])
        out[0, f, :, :HALF] = first.astype(bf16)
        out[0, f, :, HALF:] = second.astype(bf16)


def image_away(at, act_factor, grad_factor, mine, other, *outs):
    for f, factor in enumerate((act_factor, grad_factor)):
        first, second = image_rows(factor, at[0], 1 - at[1], mine, other, f, REDUCE[1:])
        for n, (group, k) in enumerate(PLACES[1:]):
            rows = slice(n * PART, (n + 1) * PART)
            outs[group - 1][k, f, :, :HALF] = first[rows].astype(bf16)
            outs[group - 1][k, f, :, HALF:] = second[rows].astype(bf16)


def image_own(at, act_factor, grad_factor, mine, other, *outs):
    for f, factor in enumerate((act_factor, grad_factor)):
        first, second = image_rows(factor, at[0], at[1], mine, other, f, REDUCE)
        for k in range(Z):
            rows = slice(k * PART, (k + 1) * PART)
            outs[k][f, :, :HALF] = first[rows]
            outs[k][f, :, HALF:] = second[rows]
        square = sum(jnp.square(part[:, factor_columns(f)].astype(f32)) for part in (mine, other))
        outs[Z][f : f + 1] = jnp.sum(square, axis=0, keepdims=True)


def last_sum(own, away, up, down, squares, out):
    total = own[...] + away[0].astype(f32) + up[...].astype(f32) + down[...].astype(f32)
    total = total.astype(bf16)
    for n in range(2 * BLOCKS):
        f, block = divmod(n, BLOCKS)
        out[n * PART : (n + 1) * PART, :] = total[f, :, block * LANES : (block + 1) * LANES]
    row = lax.broadcasted_iota(jnp.int32, (EXTRA, LANES), 0)
    parts = jnp.zeros((EXTRA, LANES), f32)
    for f in range(2):
        rest = jnp.full((EXTRA, LANES), jnp.sum(squares[f : f + 1]))
        for k in range(3):
            part = rest.astype(bf16).astype(f32)
            parts = jnp.where(row == f * EXTRA // 2 + k, part, parts)
            rest = rest - part
    out[2 * BLOCKS * PART :, :] = parts.astype(bf16)


def changes(chunks, mine, other, f):
    def image(c):
        first = f * BLOCKS
        return jnp.concatenate([c[n * PART : (n + 1) * PART, :] for n in range(first, first + BLOCKS)], axis=1)

    image = jnp.concatenate([image(c) for c in chunks], axis=0)
    change = dot(image[:, :HALF], mine[:, factor_columns(f)])
    return change + dot(image[:, HALF:], other[:, factor_columns(f)])


def own_changes(mine, other, *refs):
    chunks, (out, squares) = refs[:Z], refs[Z:]
    for f in range(2):
        out[f] = changes(chunks, mine, other, f)
        squares[f : f + 1] = share_sum(chunks, f)


def share_sum(chunks, f):
    shares = sum(c[2 * BLOCKS * PART :, :].astype(f32) for c in chunks)
    half = EXTRA // 2
    return jnp.sum(shares[f * half : (f + 1) * half], axis=0, keepdims=True)


def update(at, act_factor, grad_factor, mine, other, own_change, squares, *refs):
    chunks, outs = refs[:Z], refs[Z:]
    for f, (factor, out) in enumerate(((act_factor, outs[0]), (grad_factor, outs[1]))):
        total = squares[1 - f : 2 - f] + share_sum(chunks, 1 - f)
        scale = total[:, :1] / (TOKENS * D) * (gram_scale / TOKENS)
        for side in range(YL):
            change = own_change[f] if side == 0 else changes(chunks, mine, other, f)
            half = pl.ds(at[1] if side == 0 else 1 - at[1], 1)
            for k, e in enumerate(GATHER):
                place = (pl.ds(lax.rem(at[0] + (e + Z), Z), 1), half)
                kept = factor[place].reshape(PART, WIDTH).astype(f32)
                new = keep_scale * kept - scale * change[k * PART : (k + 1) * PART]
                out[place] = new.astype(bf16).reshape(1, 1, PART, WIDTH)


def after(a, *others):
    for other in others:
        a = a + jnp.minimum(jnp.abs(other), 0)
    return a


def local(activations, cotangents, act_factor, grad_factor):
    core, z, yl = (lax.axis_index(name) for name in ("core", "z", "yl"))
    product = 4 * HALF * ROWS * WIDTH
    given = (activations, cotangents, act_factor, grad_factor)
    scratch = [pltpu.VMEM((HALF, ROWS), bf16), pltpu.VMEM((ROWS, WIDTH), bf16)] * 2
    scratch.append(pltpu.SemaphoreType.DMA((4,)))
    setup = dict(flops=product, memory=pltpu.HBM, scratch=scratch, room=58)
    (away,) = kernel_call(project, [((HALF, 2 * WIDTH), bf16)], *given, index=[1 - core], **setup)
    came = shift(away, "core", CORE)
    (total,) = kernel_call(project_own, [((HALF, 2 * WIDTH), bf16)], *given, came, index=[core], flops=product)
    group = X * YH
    chunks = (group, HALF // group, 2 * WIDTH)
    parts = lax.all_to_all(total.reshape(chunks), ("x", "yh"), 0, 0, tiled=True)
    (copies,) = kernel_call(project_sum, [(chunks, bf16)], parts)
    mine = lax.all_to_all(copies, ("x", "yh"), 0, 0, tiled=True).reshape(HALF, 2 * WIDTH)
    other = shift(mine, "core", CORE)

    factors = [f.reshape(Z, YL, PART, WIDTH) for f in (act_factor, grad_factor)]
    shape = (2, PART, TOKENS)
    sent = [((sum(g == group for g, _ in PLACES),) + shape, bf16) for group in range(5)]
    first = kernel_call(image_first, sent[:1], *factors, mine, other, index=[z, yl], flops=product // Z)
    away = first + kernel_call(image_away, sent[1:], *factors, mine, other, index=[z, yl], flops=product)
    away = [shift(a, "yl", YL) for a in away]
    *own, squares = kernel_call(
        image_own, [(shape, f32)] * Z + [((2, WIDTH), f32)], *factors, mine, other, index=[z, yl], flops=product
    )
    up = own[0] + away[0][0].astype(f32)
    down = own[1] + away[1][0].astype(f32)
    for step in (1, 2, 3):
        up = shift(up.astype(bf16), "z", Z, 1)
        up = own[2 * step] + away[step][1].astype(f32) + up.astype(f32)
        down = shift(down.astype(bf16), "z", Z, -1)
        if step < 3:
            down = own[2 * step + 1] + away[step + 1][0].astype(f32) + down.astype(f32)
    up = shift(up.astype(bf16), "z", Z, 1)
    shape = (2 * BLOCKS * PART + EXTRA, LANES)
    (up,) = kernel_call(last_sum, [(shape, bf16)], own[7], away[4], up, down, squares)

    down = up
    held, crossed = [up], [shift(up, "yl", YL)]
    for step in (1, 2, 3):
        if step == 3:
            up, down = after(up, crossed[0]), after(down, crossed[0])
        up, down = shift(up, "z", Z, 1), shift(down, "z", Z, -1)
        held += [up, down]
        crossed += [shift(up, "yl", YL), shift(down, "yl", YL)]
    up = shift(after(up, *crossed[1:3]), "z", Z, 1)
    held.append(up)
    crossed.append(shift(up, "yl", YL))
    changed, squares = kernel_call(
        own_changes, [((2, ROWS // YL, WIDTH), f32), ((2, LANES), f32)], mine, other, *held, flops=product
    )
    outs = kernel_call(
        update, [((Z, YL, PART, WIDTH), bf16)] * 2, *factors, mine, other, changed, squares, *crossed, index=[z, yl], flops=product
    )
    return tuple(out.reshape(ROWS, WIDTH) for out in outs)


def solution(mesh):
    fine = Mesh(mesh.devices.reshape(X, YH, CORE, Z, YL), ROW + COL)
    return jax.shard_map(
        local,
        mesh=fine,
        in_specs=(P(None, ROW), P(None, ROW), P(ROW, COL), P(ROW, COL)),
        out_specs=(P(ROW, COL), P(ROW, COL)),
        check_vma=False,
    )
```

```python
import jax
import jax.numpy as jnp
from jax import lax
from jax.experimental import pallas as pl
from jax.experimental.pallas import tpu as pltpu
from jax.sharding import Mesh, PartitionSpec as P

D = 8192
TOKENS = 1024
X, YH, CORE, Z, YL = 4, 2, 2, 8, 2
ROW = ("x", "yh", "core")
COL = ("z", "yl")
ROWS = D // (X * YH * CORE)
WIDTH = D // (Z * YL)
HALF = TOKENS // CORE
EXTRA = 16
LANES = 128
BLOCKS = TOKENS // LANES
PART = ROWS // (Z * YL)

REDUCE = (4, -3, 3, -2, 2, -1, 1, 0)
PLACES = ((0, 0), (1, 0), (1, 1), (2, 0), (2, 1), (3, 0), (3, 1), (4, 0))
GATHER = (0, -1, 1, -2, 2, -3, 3, -4)

keep_scale = 1.45
gram_scale = 0.5

f32 = jnp.float32
bf16 = jnp.bfloat16


def dot(a, b):
    return jnp.dot(a, b, preferred_element_type=f32)


def dot_t(a, b):
    return lax.dot_general(a, b, (((1,), (1,)), ((), ())), preferred_element_type=f32)


def shift(a, axis, size, by=1):
    return lax.ppermute(a, axis, [(i, (i + by) % size) for i in range(size)])


def kernel_call(body, outs, *args, index=None, flops=0, memory=pltpu.VMEM, scratch=(), room=48):
    specs = [pl.BlockSpec(memory_space=memory)] * len(args)
    if index is not None:
        specs = [pl.BlockSpec(memory_space=pltpu.SMEM)] + specs
        args = (jnp.stack([i.astype(jnp.int32) for i in index]),) + args
    size = sum(a.size * a.dtype.itemsize for a in args)
    return pl.pallas_call(
        body,
        out_shape=[jax.ShapeDtypeStruct(shape, dtype) for shape, dtype in outs],
        in_specs=specs,
        out_specs=[pl.BlockSpec(memory_space=pltpu.VMEM)] * len(outs),
        scratch_shapes=scratch,
        compiler_params=pltpu.CompilerParams(vmem_limit_bytes=room * 2**20),
        cost_estimate=pl.CostEstimate(flops=flops, bytes_accessed=size, transcendentals=0),
    )(*args)


def projected(which, given, bufs, sems):
    rows = pl.ds(pl.multiple_of(which[0] * HALF, HALF), HALF)
    refs = (given[0].at[rows], given[2], given[1].at[rows], given[3])
    copies = [pltpu.make_async_copy(r, buf, sems.at[i]) for i, (r, buf) in enumerate(zip(refs, bufs))]
    for copy in copies:
        copy.start()
    for f in range(2):
        copies[2 * f].wait()
        copies[2 * f + 1].wait()
        yield f, dot(bufs[2 * f][...], bufs[2 * f + 1][...])


def project(which, acts, cots, act_factor, grad_factor, out, *scratch):
    for f, total in projected(which, (acts, cots, act_factor, grad_factor), scratch[:4], scratch[4]):
        out[:, factor_columns(f)] = total.astype(out.dtype)


def project_own(which, acts, cots, act_factor, grad_factor, came, out):
    rows = pl.ds(pl.multiple_of(which[0] * HALF, HALF), HALF)
    for f, (part, factor) in enumerate(((acts, act_factor), (cots, grad_factor))):
        cols = factor_columns(f)
        out[:, cols] = (dot(part[rows, :], factor[...]) + came[:, cols].astype(f32)).astype(bf16)


def project_sum(parts, copies):
    total = parts[0].astype(f32)
    for k in range(1, X * YH):
        total = total + parts[k].astype(f32)
    own = total.astype(bf16)
    for k in range(X * YH):
        copies[k] = own


def factor_columns(f):
    return slice(f * WIDTH, (f + 1) * WIDTH)


def image_rows(factor, z, side, chunks):
    rows = [factor[pl.ds(lax.rem(z + (e + Z), Z), 1), pl.ds(side, 1)].reshape(PART, WIDTH) for e in chunks]
    return jnp.concatenate(rows, axis=0)


def image_first(at, act_factor, grad_factor, mine, other, *outs):
    for f, factor in enumerate((act_factor, grad_factor)):
        rows = image_rows(factor, at[0], 1 - at[1], REDUCE[:4])
        for part, cols in ((mine, slice(0, HALF)), (other, slice(HALF, TOKENS))):
            image = dot_t(part[:, factor_columns(f)], rows).T.astype(bf16)
            for n, (group, k) in enumerate(PLACES[:3]):
                outs[group][k, f, :, cols] = image[n * PART : (n + 1) * PART]


def image_away(at, act_factor, grad_factor, mine, other, *outs):
    for f, factor in enumerate((act_factor, grad_factor)):
        rows = image_rows(factor, at[0], 1 - at[1], REDUCE[3:])
        for part, cols in ((mine, slice(0, HALF)), (other, slice(HALF, TOKENS))):
            image = dot_t(rows, part[:, factor_columns(f)]).astype(bf16)
            for n, (group, k) in enumerate(PLACES[3:]):
                outs[group - 2][k, f, :, cols] = image[n * PART : (n + 1) * PART]


def image_own(at, act_factor, grad_factor, mine, other, *outs):
    for f, factor in enumerate((act_factor, grad_factor)):
        rows = image_rows(factor, at[0], at[1], REDUCE)
        for part, cols in ((mine, slice(0, HALF)), (other, slice(HALF, TOKENS))):
            image = dot_t(rows, part[:, factor_columns(f)])
            for k in range(Z):
                outs[k][f, :, cols] = image[k * PART : (k + 1) * PART]
        square = sum(jnp.square(part[:, factor_columns(f)].astype(f32)) for part in (mine, other))
        outs[Z][f : f + 1] = jnp.sum(square, axis=0, keepdims=True)


def last_sum(own, away, up, down, squares, out):
    total = own[...] + away[0].astype(f32) + up[...].astype(f32) + down[...].astype(f32)
    total = total.astype(bf16)
    for n in range(2 * BLOCKS):
        f, block = divmod(n, BLOCKS)
        out[n * PART : (n + 1) * PART, :] = total[f, :, block * LANES : (block + 1) * LANES]
    row = lax.broadcasted_iota(jnp.int32, (EXTRA, LANES), 0)
    parts = jnp.zeros((EXTRA, LANES), f32)
    for f in range(2):
        rest = jnp.full((EXTRA, LANES), jnp.sum(squares[f : f + 1]))
        for k in range(3):
            part = rest.astype(bf16).astype(f32)
            parts = jnp.where(row == f * EXTRA // 2 + k, part, parts)
            rest = rest - part
    out[2 * BLOCKS * PART :, :] = parts.astype(bf16)


def changes(chunks, mine, other, f):
    def image(c):
        first = f * BLOCKS
        return jnp.concatenate([c[n * PART : (n + 1) * PART, :] for n in range(first, first + BLOCKS)], axis=1)

    image = jnp.concatenate([image(c) for c in chunks], axis=0)
    change = dot(image[:, :HALF], mine[:, factor_columns(f)])
    return change + dot(image[:, HALF:], other[:, factor_columns(f)])


def own_changes(mine, other, *refs):
    chunks, (out, squares) = refs[:Z], refs[Z:]
    for f in range(2):
        out[f] = changes(chunks, mine, other, f)
        squares[f : f + 1] = share_sum(chunks, f)


def share_sum(chunks, f):
    shares = sum(c[2 * BLOCKS * PART :, :].astype(f32) for c in chunks)
    half = EXTRA // 2
    return jnp.sum(shares[f * half : (f + 1) * half], axis=0, keepdims=True)


def update(at, act_factor, grad_factor, mine, other, own_change, squares, *refs):
    chunks, outs = refs[:Z], refs[Z:]
    for f, (factor, out) in enumerate(((act_factor, outs[0]), (grad_factor, outs[1]))):
        total = squares[1 - f : 2 - f] + share_sum(chunks, 1 - f)
        scale = total[:, :1] / (TOKENS * D) * (gram_scale / TOKENS)
        for side in range(YL):
            change = own_change[f] if side == 0 else changes(chunks, mine, other, f)
            half = pl.ds(at[1] if side == 0 else 1 - at[1], 1)
            for k, e in enumerate(GATHER):
                place = (pl.ds(lax.rem(at[0] + (e + Z), Z), 1), half)
                kept = factor[place].reshape(PART, WIDTH).astype(f32)
                new = keep_scale * kept - scale * change[k * PART : (k + 1) * PART]
                out[place] = new.astype(bf16).reshape(1, 1, PART, WIDTH)


def after(a, *others):
    for other in others:
        a = a + jnp.minimum(jnp.abs(other), 0)
    return a


def local(activations, cotangents, act_factor, grad_factor):
    core, z, yl = (lax.axis_index(name) for name in ("core", "z", "yl"))
    product = 4 * HALF * ROWS * WIDTH
    given = (activations, cotangents, act_factor, grad_factor)
    scratch = [pltpu.VMEM((HALF, ROWS), bf16), pltpu.VMEM((ROWS, WIDTH), bf16)] * 2
    scratch.append(pltpu.SemaphoreType.DMA((4,)))
    setup = dict(flops=product, memory=pltpu.HBM, scratch=scratch, room=58)
    (away,) = kernel_call(project, [((HALF, 2 * WIDTH), bf16)], *given, index=[1 - core], **setup)
    came = shift(away, "core", CORE)
    (total,) = kernel_call(project_own, [((HALF, 2 * WIDTH), bf16)], *given, came, index=[core], flops=product)
    group = X * YH
    chunks = (group, HALF // group, 2 * WIDTH)
    parts = lax.all_to_all(total.reshape(chunks), ("x", "yh"), 0, 0, tiled=True)
    (copies,) = kernel_call(project_sum, [(chunks, bf16)], parts)
    mine = lax.all_to_all(copies, ("x", "yh"), 0, 0, tiled=True).reshape(HALF, 2 * WIDTH)
    other = shift(mine, "core", CORE)

    factors = [f.reshape(Z, YL, PART, WIDTH) for f in (act_factor, grad_factor)]
    shape = (2, PART, TOKENS)
    sent = [((sum(g == group for g, _ in PLACES),) + shape, bf16) for group in range(5)]
    first = kernel_call(image_first, sent[:2], *factors, mine, other, index=[z, yl], flops=product // 2)
    away = first + kernel_call(image_away, sent[2:], *factors, mine, other, index=[z, yl], flops=product)
    away = [shift(a, "yl", YL) for a in away]
    *own, squares = kernel_call(
        image_own, [(shape, f32)] * Z + [((2, WIDTH), f32)], *factors, mine, other, index=[z, yl], flops=product
    )
    up = own[0] + away[0][0].astype(f32)
    down = own[1] + away[1][0].astype(f32)
    for step in (1, 2, 3):
        up = shift(up.astype(bf16), "z", Z, 1)
        up = own[2 * step] + away[step][1].astype(f32) + up.astype(f32)
        down = shift(down.astype(bf16), "z", Z, -1)
        if step < 3:
            down = own[2 * step + 1] + away[step + 1][0].astype(f32) + down.astype(f32)
    up = shift(up.astype(bf16), "z", Z, 1)
    shape = (2 * BLOCKS * PART + EXTRA, LANES)
    (up,) = kernel_call(last_sum, [(shape, bf16)], own[7], away[4], up, down, squares)

    down = up
    held, crossed = [up], [shift(up, "yl", YL)]
    for step in (1, 2, 3):
        if step == 3:
            up, down = after(up, crossed[0]), after(down, crossed[0])
        up, down = shift(up, "z", Z, 1), shift(down, "z", Z, -1)
        held += [up, down]
        crossed += [shift(up, "yl", YL), shift(down, "yl", YL)]
    up = shift(after(up, *crossed[1:3]), "z", Z, 1)
    held.append(up)
    crossed.append(shift(up, "yl", YL))
    changed, squares = kernel_call(
        own_changes, [((2, ROWS // YL, WIDTH), f32), ((2, LANES), f32)], mine, other, *held, flops=product
    )
    outs = kernel_call(
        update, [((Z, YL, PART, WIDTH), bf16)] * 2, *factors, mine, other, changed, squares, *crossed, index=[z, yl], flops=product
    )
    return tuple(out.reshape(ROWS, WIDTH) for out in outs)


def solution(mesh):
    fine = Mesh(mesh.devices.reshape(X, YH, CORE, Z, YL), ROW + COL)
    return jax.shard_map(
        local,
        mesh=fine,
        in_specs=(P(None, ROW), P(None, ROW), P(ROW, COL), P(ROW, COL)),
        out_specs=(P(ROW, COL), P(ROW, COL)),
        check_vma=False,
    )
```

```python
import jax
import jax.numpy as jnp
from jax import lax
from jax.experimental import pallas as pl
from jax.experimental.pallas import tpu as pltpu
from jax.sharding import Mesh, PartitionSpec as P

D = 8192
TOKENS = 1024
X, YH, CORE, Z, YL = 4, 2, 2, 8, 2
ROW = ("x", "yh", "core")
COL = ("z", "yl")
ROWS = D // (X * YH * CORE)
WIDTH = D // (Z * YL)
HALF = TOKENS // CORE
EXTRA = 16
LANES = 128
BLOCKS = TOKENS // LANES
PART = ROWS // (Z * YL)

REDUCE = (4, -3, 3, -2, 2, -1, 1, 0)
PLACES = ((0, 0), (1, 0), (1, 1), (2, 0), (2, 1), (3, 0), (3, 1), (4, 0))
GATHER = (0, -1, 1, -2, 2, -3, 3, -4)

keep_scale = 1.45
gram_scale = 0.5

f32 = jnp.float32
bf16 = jnp.bfloat16


def dot(a, b):
    return jnp.dot(a, b, preferred_element_type=f32)


def dot_t(a, b):
    return lax.dot_general(a, b, (((1,), (1,)), ((), ())), preferred_element_type=f32)


def shift(a, axis, size, by=1):
    return lax.ppermute(a, axis, [(i, (i + by) % size) for i in range(size)])


def kernel_call(body, outs, *args, index=None, flops=0, memory=pltpu.VMEM, scratch=(), room=48):
    specs = [pl.BlockSpec(memory_space=memory)] * len(args)
    if index is not None:
        specs = [pl.BlockSpec(memory_space=pltpu.SMEM)] + specs
        args = (jnp.stack([i.astype(jnp.int32) for i in index]),) + args
    size = sum(a.size * a.dtype.itemsize for a in args)
    return pl.pallas_call(
        body,
        out_shape=[jax.ShapeDtypeStruct(shape, dtype) for shape, dtype in outs],
        in_specs=specs,
        out_specs=[pl.BlockSpec(memory_space=pltpu.VMEM)] * len(outs),
        scratch_shapes=scratch,
        compiler_params=pltpu.CompilerParams(vmem_limit_bytes=room * 2**20),
        cost_estimate=pl.CostEstimate(flops=flops, bytes_accessed=size, transcendentals=0),
    )(*args)


def projected(which, given, bufs, sems):
    rows = pl.ds(pl.multiple_of(which[0] * HALF, HALF), HALF)
    refs = (given[0].at[rows], given[2], given[1].at[rows], given[3])
    copies = [pltpu.make_async_copy(r, buf, sems.at[i]) for i, (r, buf) in enumerate(zip(refs, bufs))]
    for copy in copies:
        copy.start()
    for f in range(2):
        copies[2 * f].wait()
        copies[2 * f + 1].wait()
        yield f, dot(bufs[2 * f][...], bufs[2 * f + 1][...])


def project(which, acts, cots, act_factor, grad_factor, out, *scratch):
    for f, total in projected(which, (acts, cots, act_factor, grad_factor), scratch[:4], scratch[4]):
        out[:, factor_columns(f)] = total.astype(out.dtype)


def project_own(which, acts, cots, act_factor, grad_factor, came, out):
    rows = pl.ds(pl.multiple_of(which[0] * HALF, HALF), HALF)
    for f, (part, factor) in enumerate(((acts, act_factor), (cots, grad_factor))):
        cols = factor_columns(f)
        out[:, cols] = (dot(part[rows, :], factor[...]) + came[:, cols].astype(f32)).astype(bf16)


def project_sum(parts, copies):
    total = parts[0].astype(f32)
    for k in range(1, X * YH):
        total = total + parts[k].astype(f32)
    own = total.astype(bf16)
    for k in range(X * YH):
        copies[k] = own


def factor_columns(f):
    return slice(f * WIDTH, (f + 1) * WIDTH)


def image_rows(factor, z, side, chunks):
    rows = [factor[pl.ds(lax.rem(z + (e + Z), Z), 1), pl.ds(side, 1)].reshape(PART, WIDTH) for e in chunks]
    return jnp.concatenate(rows, axis=0)


def image_first(at, act_factor, grad_factor, mine, other, *outs):
    for f, factor in enumerate((act_factor, grad_factor)):
        rows = image_rows(factor, at[0], 1 - at[1], REDUCE[:4])
        for part, cols in ((mine, slice(0, HALF)), (other, slice(HALF, TOKENS))):
            image = dot_t(part[:, factor_columns(f)], rows).T.astype(bf16)
            for n, (group, k) in enumerate(PLACES[:3]):
                outs[group][k, f, :, cols] = image[n * PART : (n + 1) * PART]


def image_away(at, act_factor, grad_factor, mine, other, *outs):
    for f, factor in enumerate((act_factor, grad_factor)):
        rows = image_rows(factor, at[0], 1 - at[1], REDUCE[3:])
        for part, cols in ((mine, slice(0, HALF)), (other, slice(HALF, TOKENS))):
            image = dot_t(rows, part[:, factor_columns(f)]).astype(bf16)
            for n, (group, k) in enumerate(PLACES[3:]):
                outs[group - 2][k, f, :, cols] = image[n * PART : (n + 1) * PART]


def image_own(at, act_factor, grad_factor, mine, other, *outs):
    for f, factor in enumerate((act_factor, grad_factor)):
        rows = image_rows(factor, at[0], at[1], REDUCE)
        for part, cols in ((mine, slice(0, HALF)), (other, slice(HALF, TOKENS))):
            image = dot_t(rows, part[:, factor_columns(f)])
            for k in range(Z):
                outs[k][f, :, cols] = image[k * PART : (k + 1) * PART]
        square = sum(jnp.square(part[:, factor_columns(f)].astype(f32)) for part in (mine, other))
        outs[Z][f : f + 1] = jnp.sum(square, axis=0, keepdims=True)


def last_sum(own, away, up, down, squares, out):
    total = own[...] + away[0].astype(f32) + up[...].astype(f32) + down[...].astype(f32)
    total = total.astype(bf16)
    for n in range(2 * BLOCKS):
        f, block = divmod(n, BLOCKS)
        out[n * PART : (n + 1) * PART, :] = total[f, :, block * LANES : (block + 1) * LANES]
    row = lax.broadcasted_iota(jnp.int32, (EXTRA, LANES), 0)
    parts = jnp.zeros((EXTRA, LANES), f32)
    for f in range(2):
        rest = jnp.full((EXTRA, LANES), jnp.sum(squares[f : f + 1]))
        for k in range(3):
            part = rest.astype(bf16).astype(f32)
            parts = jnp.where(row == f * EXTRA // 2 + k, part, parts)
            rest = rest - part
    out[2 * BLOCKS * PART :, :] = parts.astype(bf16)


def changes(chunks, mine, other, f):
    def image(c):
        first = f * BLOCKS
        return jnp.concatenate([c[n * PART : (n + 1) * PART, :] for n in range(first, first + BLOCKS)], axis=1)

    image = jnp.concatenate([image(c) for c in chunks], axis=0)
    change = dot(image[:, :HALF], mine[:, factor_columns(f)])
    return change + dot(image[:, HALF:], other[:, factor_columns(f)])


def own_changes(mine, other, *refs):
    chunks, (out, squares) = refs[:Z], refs[Z:]
    for f in range(2):
        out[f] = changes(chunks, mine, other, f)
        squares[f : f + 1] = share_sum(chunks, f)


def share_sum(chunks, f):
    shares = sum(c[2 * BLOCKS * PART :, :].astype(f32) for c in chunks)
    half = EXTRA // 2
    return jnp.sum(shares[f * half : (f + 1) * half], axis=0, keepdims=True)


def update(at, act_factor, grad_factor, mine, other, own_change, squares, *refs):
    chunks, outs = refs[:-2], refs[-2:]
    chunks = [*chunks[:3], chunks[3].at[0], chunks[3].at[1], *chunks[4:]]
    for f, (factor, out) in enumerate(((act_factor, outs[0]), (grad_factor, outs[1]))):
        total = squares[1 - f : 2 - f] + share_sum(chunks, 1 - f)
        scale = total[:, :1] / (TOKENS * D) * (gram_scale / TOKENS)
        for side in range(YL):
            change = own_change[f] if side == 0 else changes(chunks, mine, other, f)
            half = pl.ds(at[1] if side == 0 else 1 - at[1], 1)
            for k, e in enumerate(GATHER):
                place = (pl.ds(lax.rem(at[0] + (e + Z), Z), 1), half)
                kept = factor[place].reshape(PART, WIDTH).astype(f32)
                new = keep_scale * kept - scale * change[k * PART : (k + 1) * PART]
                out[place] = new.astype(bf16).reshape(1, 1, PART, WIDTH)


def after(a, *others):
    for other in others:
        a = a + jnp.minimum(jnp.abs(other), 0)
    return a


def local(activations, cotangents, act_factor, grad_factor):
    core, z, yl = (lax.axis_index(name) for name in ("core", "z", "yl"))
    product = 4 * HALF * ROWS * WIDTH
    given = (activations, cotangents, act_factor, grad_factor)
    scratch = [pltpu.VMEM((HALF, ROWS), bf16), pltpu.VMEM((ROWS, WIDTH), bf16)] * 2
    scratch.append(pltpu.SemaphoreType.DMA((4,)))
    setup = dict(flops=product, memory=pltpu.HBM, scratch=scratch, room=58)
    (away,) = kernel_call(project, [((HALF, 2 * WIDTH), bf16)], *given, index=[1 - core], **setup)
    came = shift(away, "core", CORE)
    (total,) = kernel_call(project_own, [((HALF, 2 * WIDTH), bf16)], *given, came, index=[core], flops=product)
    group = X * YH
    chunks = (group, HALF // group, 2 * WIDTH)
    parts = lax.all_to_all(total.reshape(chunks), ("x", "yh"), 0, 0, tiled=True)
    (copies,) = kernel_call(project_sum, [(chunks, bf16)], parts)
    mine = lax.all_to_all(copies, ("x", "yh"), 0, 0, tiled=True).reshape(HALF, 2 * WIDTH)
    other = shift(mine, "core", CORE)

    factors = [f.reshape(Z, YL, PART, WIDTH) for f in (act_factor, grad_factor)]
    shape = (2, PART, TOKENS)
    sent = [((sum(g == group for g, _ in PLACES),) + shape, bf16) for group in range(5)]
    first = kernel_call(image_first, sent[:2], *factors, mine, other, index=[z, yl], flops=product // 2)
    away = first + kernel_call(image_away, sent[2:], *factors, mine, other, index=[z, yl], flops=product)
    away = [shift(a, "yl", YL) for a in away]
    *own, squares = kernel_call(
        image_own, [(shape, f32)] * Z + [((2, WIDTH), f32)], *factors, mine, other, index=[z, yl], flops=product
    )
    up = own[0] + away[0][0].astype(f32)
    down = own[1] + away[1][0].astype(f32)
    for step in (1, 2, 3):
        up = shift(up.astype(bf16), "z", Z, 1)
        up = own[2 * step] + away[step][1].astype(f32) + up.astype(f32)
        down = shift(down.astype(bf16), "z", Z, -1)
        if step < 3:
            down = own[2 * step + 1] + away[step + 1][0].astype(f32) + down.astype(f32)
    up = shift(up.astype(bf16), "z", Z, 1)
    shape = (2 * BLOCKS * PART + EXTRA, LANES)
    (up,) = kernel_call(last_sum, [(shape, bf16)], own[7], away[4], up, down, squares)

    down = up
    held, crossed = [up], [shift(up, "yl", YL)]
    for step in (1, 2, 3):
        if step == 3:
            up, down = after(up, crossed[0]), after(down, crossed[0])
        up, down = shift(up, "z", Z, 1), shift(down, "z", Z, -1)
        held += [up, down]
        if step == 2:
            crossed.append(shift(jnp.stack([up, down]), "yl", YL))
        else:
            crossed += [shift(up, "yl", YL), shift(down, "yl", YL)]
    up = shift(after(up, *crossed[1:3]), "z", Z, 1)
    held.append(up)
    crossed.append(shift(up, "yl", YL))
    changed, squares = kernel_call(
        own_changes, [((2, ROWS // YL, WIDTH), f32), ((2, LANES), f32)], mine, other, *held, flops=product
    )
    outs = kernel_call(
        update, [((Z, YL, PART, WIDTH), bf16)] * 2, *factors, mine, other, changed, squares, *crossed, index=[z, yl], flops=product
    )
    return tuple(out.reshape(ROWS, WIDTH) for out in outs)


def solution(mesh):
    fine = Mesh(mesh.devices.reshape(X, YH, CORE, Z, YL), ROW + COL)
    return jax.shard_map(
        local,
        mesh=fine,
        in_specs=(P(None, ROW), P(None, ROW), P(ROW, COL), P(ROW, COL)),
        out_specs=(P(ROW, COL), P(ROW, COL)),
        check_vma=False,
    )
```

```python
import jax
import jax.numpy as jnp
from jax import lax
from jax.experimental import pallas as pl
from jax.experimental.pallas import tpu as pltpu
from jax.sharding import Mesh, PartitionSpec as P

D = 8192
TOKENS = 1024
X, YH, CORE, Z, YL = 4, 2, 2, 8, 2
ROW = ("x", "yh", "core")
COL = ("z", "yl")
ROWS = D // (X * YH * CORE)
WIDTH = D // (Z * YL)
HALF = TOKENS // CORE
EXTRA = 16
LANES = 128
BLOCKS = TOKENS // LANES
PART = ROWS // (Z * YL)

REDUCE = (4, -3, 3, -2, 2, -1, 1, 0)
PLACES = ((0, 0), (1, 0), (1, 1), (2, 0), (2, 1), (3, 0), (3, 1), (4, 0))
GATHER = (0, -1, 1, -2, 2, -3, 3, -4)

keep_scale = 1.45
gram_scale = 0.5

f32 = jnp.float32
bf16 = jnp.bfloat16


def dot(a, b):
    return jnp.dot(a, b, preferred_element_type=f32)


def dot_t(a, b):
    return lax.dot_general(a, b, (((1,), (1,)), ((), ())), preferred_element_type=f32)


def shift(a, axis, size, by=1):
    return lax.ppermute(a, axis, [(i, (i + by) % size) for i in range(size)])


def kernel_call(body, outs, *args, index=None, flops=0, memory=pltpu.VMEM, scratch=(), room=48):
    specs = [pl.BlockSpec(memory_space=memory)] * len(args)
    if index is not None:
        specs = [pl.BlockSpec(memory_space=pltpu.SMEM)] + specs
        args = (jnp.stack([i.astype(jnp.int32) for i in index]),) + args
    size = sum(a.size * a.dtype.itemsize for a in args)
    return pl.pallas_call(
        body,
        out_shape=[jax.ShapeDtypeStruct(shape, dtype) for shape, dtype in outs],
        in_specs=specs,
        out_specs=[pl.BlockSpec(memory_space=pltpu.VMEM)] * len(outs),
        scratch_shapes=scratch,
        compiler_params=pltpu.CompilerParams(vmem_limit_bytes=room * 2**20),
        cost_estimate=pl.CostEstimate(flops=flops, bytes_accessed=size, transcendentals=0),
    )(*args)


def projected(which, given, bufs, sems):
    rows = pl.ds(pl.multiple_of(which[0] * HALF, HALF), HALF)
    refs = (given[0].at[rows], given[2], given[1].at[rows], given[3])
    copies = [pltpu.make_async_copy(r, buf, sems.at[i]) for i, (r, buf) in enumerate(zip(refs, bufs))]
    for copy in copies:
        copy.start()
    for f in range(2):
        copies[2 * f].wait()
        copies[2 * f + 1].wait()
        yield f, dot(bufs[2 * f][...], bufs[2 * f + 1][...])


def project(which, acts, cots, act_factor, grad_factor, out, *scratch):
    for f, total in projected(which, (acts, cots, act_factor, grad_factor), scratch[:4], scratch[4]):
        out[:, factor_columns(f)] = total.astype(out.dtype)


def project_own(which, acts, cots, act_factor, grad_factor, came, out):
    rows = pl.ds(pl.multiple_of(which[0] * HALF, HALF), HALF)
    for f, (part, factor) in enumerate(((acts, act_factor), (cots, grad_factor))):
        cols = factor_columns(f)
        out[:, cols] = (dot(part[rows, :], factor[...]) + came[:, cols].astype(f32)).astype(bf16)


def project_sum(parts, copies):
    total = parts[0].astype(f32)
    for k in range(1, X * YH):
        total = total + parts[k].astype(f32)
    own = total.astype(bf16)
    for k in range(X * YH):
        copies[k] = own


def factor_columns(f):
    return slice(f * WIDTH, (f + 1) * WIDTH)


def image_rows(factor, z, side, chunks):
    rows = [factor[pl.ds(lax.rem(z + (e + Z), Z), 1), pl.ds(side, 1)].reshape(PART, WIDTH) for e in chunks]
    return jnp.concatenate(rows, axis=0)


def image_first(at, act_factor, grad_factor, mine, other, *outs):
    for f, factor in enumerate((act_factor, grad_factor)):
        rows = image_rows(factor, at[0], 1 - at[1], REDUCE[:4])
        for part, cols in ((mine, slice(0, HALF)), (other, slice(HALF, TOKENS))):
            image = dot_t(part[:, factor_columns(f)], rows).T.astype(bf16)
            for n, (group, k) in enumerate(PLACES[:3]):
                outs[group][k, f, :, cols] = image[n * PART : (n + 1) * PART]


def image_away(at, act_factor, grad_factor, mine, other, *outs):
    for f, factor in enumerate((act_factor, grad_factor)):
        rows = image_rows(factor, at[0], 1 - at[1], REDUCE[3:])
        for part, cols in ((mine, slice(0, HALF)), (other, slice(HALF, TOKENS))):
            image = dot_t(rows, part[:, factor_columns(f)]).astype(bf16)
            for n, (group, k) in enumerate(PLACES[3:]):
                outs[group - 2][k, f, :, cols] = image[n * PART : (n + 1) * PART]


def image_own(at, act_factor, grad_factor, mine, other, *outs):
    for f, factor in enumerate((act_factor, grad_factor)):
        rows = image_rows(factor, at[0], at[1], REDUCE)
        for part, cols in ((mine, slice(0, HALF)), (other, slice(HALF, TOKENS))):
            image = dot_t(rows, part[:, factor_columns(f)])
            for k in range(Z):
                outs[k][f, :, cols] = image[k * PART : (k + 1) * PART]
        square = sum(jnp.square(part[:, factor_columns(f)].astype(f32)) for part in (mine, other))
        outs[Z][f : f + 1] = jnp.sum(square, axis=0, keepdims=True)


def last_sum(own, away, up, down, squares, out):
    total = own[...] + away[0].astype(f32) + up[...].astype(f32) + down[...].astype(f32)
    total = total.astype(bf16)
    for n in range(2 * BLOCKS):
        f, block = divmod(n, BLOCKS)
        out[n * PART : (n + 1) * PART, :] = total[f, :, block * LANES : (block + 1) * LANES]
    row = lax.broadcasted_iota(jnp.int32, (EXTRA, LANES), 0)
    parts = jnp.zeros((EXTRA, LANES), f32)
    for f in range(2):
        rest = jnp.full((EXTRA, LANES), jnp.sum(squares[f : f + 1]))
        for k in range(3):
            part = rest.astype(bf16).astype(f32)
            parts = jnp.where(row == f * EXTRA // 2 + k, part, parts)
            rest = rest - part
    out[2 * BLOCKS * PART :, :] = parts.astype(bf16)


def changes(chunks, mine, other, f):
    def image(c):
        first = f * BLOCKS
        return jnp.concatenate([c[n * PART : (n + 1) * PART, :] for n in range(first, first + BLOCKS)], axis=1)

    image = jnp.concatenate([image(c) for c in chunks], axis=0)
    change = dot(image[:, :HALF], mine[:, factor_columns(f)])
    return change + dot(image[:, HALF:], other[:, factor_columns(f)])


def own_changes(mine, other, *refs):
    chunks, (out, squares) = refs[:Z], refs[Z:]
    for f in range(2):
        out[f] = changes(chunks, mine, other, f)
        squares[f : f + 1] = share_sum(chunks, f)


def share_sum(chunks, f):
    shares = sum(c[2 * BLOCKS * PART :, :].astype(f32) for c in chunks)
    half = EXTRA // 2
    return jnp.sum(shares[f * half : (f + 1) * half], axis=0, keepdims=True)


def update(at, act_factor, grad_factor, mine, other, own_change, squares, *refs):
    chunks, outs = refs[:-2], refs[-2:]
    chunks = [chunks[0], *(pair.at[k] for pair in chunks[1:3] for k in range(2)), *chunks[3:]]
    for f, (factor, out) in enumerate(((act_factor, outs[0]), (grad_factor, outs[1]))):
        total = squares[1 - f : 2 - f] + share_sum(chunks, 1 - f)
        scale = total[:, :1] / (TOKENS * D) * (gram_scale / TOKENS)
        for side in range(YL):
            change = own_change[f] if side == 0 else changes(chunks, mine, other, f)
            half = pl.ds(at[1] if side == 0 else 1 - at[1], 1)
            for k, e in enumerate(GATHER):
                place = (pl.ds(lax.rem(at[0] + (e + Z), Z), 1), half)
                kept = factor[place].reshape(PART, WIDTH).astype(f32)
                new = keep_scale * kept - scale * change[k * PART : (k + 1) * PART]
                out[place] = new.astype(bf16).reshape(1, 1, PART, WIDTH)


def after(a, *others):
    for other in others:
        a = a + jnp.minimum(jnp.abs(other), 0)
    return a


def local(activations, cotangents, act_factor, grad_factor):
    core, z, yl = (lax.axis_index(name) for name in ("core", "z", "yl"))
    product = 4 * HALF * ROWS * WIDTH
    given = (activations, cotangents, act_factor, grad_factor)
    scratch = [pltpu.VMEM((HALF, ROWS), bf16), pltpu.VMEM((ROWS, WIDTH), bf16)] * 2
    scratch.append(pltpu.SemaphoreType.DMA((4,)))
    setup = dict(flops=product, memory=pltpu.HBM, scratch=scratch, room=58)
    (away,) = kernel_call(project, [((HALF, 2 * WIDTH), bf16)], *given, index=[1 - core], **setup)
    came = shift(away, "core", CORE)
    (total,) = kernel_call(project_own, [((HALF, 2 * WIDTH), bf16)], *given, came, index=[core], flops=product)
    group = X * YH
    chunks = (group, HALF // group, 2 * WIDTH)
    parts = lax.all_to_all(total.reshape(chunks), ("x", "yh"), 0, 0, tiled=True)
    (copies,) = kernel_call(project_sum, [(chunks, bf16)], parts)
    mine = lax.all_to_all(copies, ("x", "yh"), 0, 0, tiled=True).reshape(HALF, 2 * WIDTH)
    other = shift(mine, "core", CORE)

    factors = [f.reshape(Z, YL, PART, WIDTH) for f in (act_factor, grad_factor)]
    shape = (2, PART, TOKENS)
    sent = [((sum(g == group for g, _ in PLACES),) + shape, bf16) for group in range(5)]
    first = kernel_call(image_first, sent[:2], *factors, mine, other, index=[z, yl], flops=product // 2)
    away = first + kernel_call(image_away, sent[2:], *factors, mine, other, index=[z, yl], flops=product)
    away = [shift(a, "yl", YL) for a in away]
    *own, squares = kernel_call(
        image_own, [(shape, f32)] * Z + [((2, WIDTH), f32)], *factors, mine, other, index=[z, yl], flops=product
    )
    up = own[0] + away[0][0].astype(f32)
    down = own[1] + away[1][0].astype(f32)
    for step in (1, 2, 3):
        up = shift(up.astype(bf16), "z", Z, 1)
        up = own[2 * step] + away[step][1].astype(f32) + up.astype(f32)
        down = shift(down.astype(bf16), "z", Z, -1)
        if step < 3:
            down = own[2 * step + 1] + away[step + 1][0].astype(f32) + down.astype(f32)
    up = shift(up.astype(bf16), "z", Z, 1)
    shape = (2 * BLOCKS * PART + EXTRA, LANES)
    (up,) = kernel_call(last_sum, [(shape, bf16)], own[7], away[4], up, down, squares)

    down = up
    held, crossed = [up], [shift(up, "yl", YL)]
    for step in (1, 2, 3):
        if step == 3:
            up, down = after(up, crossed[0]), after(down, crossed[0])
        up, down = shift(up, "z", Z, 1), shift(down, "z", Z, -1)
        held += [up, down]
        if step < 3:
            crossed.append(shift(jnp.stack([up, down]), "yl", YL))
        else:
            crossed += [shift(up, "yl", YL), shift(down, "yl", YL)]
    up = shift(after(up, crossed[1][0]), "z", Z, 1)
    held.append(up)
    crossed.append(shift(up, "yl", YL))
    changed, squares = kernel_call(
        own_changes, [((2, ROWS // YL, WIDTH), f32), ((2, LANES), f32)], mine, other, *held, flops=product
    )
    outs = kernel_call(
        update, [((Z, YL, PART, WIDTH), bf16)] * 2, *factors, mine, other, changed, squares, *crossed, index=[z, yl], flops=product
    )
    return tuple(out.reshape(ROWS, WIDTH) for out in outs)


def solution(mesh):
    fine = Mesh(mesh.devices.reshape(X, YH, CORE, Z, YL), ROW + COL)
    return jax.shard_map(
        local,
        mesh=fine,
        in_specs=(P(None, ROW), P(None, ROW), P(ROW, COL), P(ROW, COL)),
        out_specs=(P(ROW, COL), P(ROW, COL)),
        check_vma=False,
    )
```

```python
import jax
import jax.numpy as jnp
from jax import lax
from jax.experimental import pallas as pl
from jax.experimental.pallas import tpu as pltpu
from jax.sharding import Mesh, PartitionSpec as P

D = 8192
TOKENS = 1024
X, YH, CORE, Z, YL = 4, 2, 2, 8, 2
ROW = ("x", "yh", "core")
COL = ("z", "yl")
ROWS = D // (X * YH * CORE)
WIDTH = D // (Z * YL)
HALF = TOKENS // CORE
EXTRA = 16
LANES = 128
BLOCKS = TOKENS // LANES
PART = ROWS // (Z * YL)

REDUCE = (4, -3, 3, -2, 2, -1, 1, 0)
PLACES = ((0, 0), (1, 0), (1, 1), (2, 0), (2, 1), (3, 0), (3, 1), (4, 0))
GATHER = (0, -1, 1, -2, 2, -3, 3, -4)

keep_scale = 1.45
gram_scale = 0.5

f32 = jnp.float32
bf16 = jnp.bfloat16


def dot(a, b):
    return jnp.dot(a, b, preferred_element_type=f32)


def dot_t(a, b):
    return lax.dot_general(a, b, (((1,), (1,)), ((), ())), preferred_element_type=f32)


def shift(a, axis, size, by=1):
    return lax.ppermute(a, axis, [(i, (i + by) % size) for i in range(size)])


def kernel_call(body, outs, *args, index=None, flops=0, memory=pltpu.VMEM, out_memory=pltpu.VMEM, scratch=(), room=48):
    specs = [pl.BlockSpec(memory_space=memory)] * len(args)
    if index is not None:
        specs = [pl.BlockSpec(memory_space=pltpu.SMEM)] + specs
        args = (jnp.stack([i.astype(jnp.int32) for i in index]),) + args
    size = sum(a.size * a.dtype.itemsize for a in args)
    return pl.pallas_call(
        body,
        out_shape=[jax.ShapeDtypeStruct(shape, dtype) for shape, dtype in outs],
        in_specs=specs,
        out_specs=[pl.BlockSpec(memory_space=out_memory)] * len(outs),
        scratch_shapes=scratch,
        compiler_params=pltpu.CompilerParams(vmem_limit_bytes=room * 2**20),
        cost_estimate=pl.CostEstimate(flops=flops, bytes_accessed=size, transcendentals=0),
    )(*args)


def projected(which, given, bufs, sems):
    rows = pl.ds(pl.multiple_of(which[0] * HALF, HALF), HALF)
    refs = (given[0].at[rows], given[2], given[1].at[rows], given[3])
    copies = [pltpu.make_async_copy(r, buf, sems.at[i]) for i, (r, buf) in enumerate(zip(refs, bufs))]
    for copy in copies:
        copy.start()
    for f in range(2):
        copies[2 * f].wait()
        copies[2 * f + 1].wait()
        yield f, dot(bufs[2 * f][...], bufs[2 * f + 1][...])


def project(which, acts, cots, act_factor, grad_factor, out, *scratch):
    for f, total in projected(which, (acts, cots, act_factor, grad_factor), scratch[:4], scratch[4]):
        out[:, factor_columns(f)] = total.astype(out.dtype)


def project_own(which, acts, cots, act_factor, grad_factor, came, out):
    rows = pl.ds(pl.multiple_of(which[0] * HALF, HALF), HALF)
    for f, (part, factor) in enumerate(((acts, act_factor), (cots, grad_factor))):
        cols = factor_columns(f)
        out[:, cols] = (dot(part[rows, :], factor[...]) + came[:, cols].astype(f32)).astype(bf16)


def project_sum(parts, copies):
    total = parts[0].astype(f32)
    for k in range(1, X * YH):
        total = total + parts[k].astype(f32)
    own = total.astype(bf16)
    for k in range(X * YH):
        copies[k] = own


def factor_columns(f):
    return slice(f * WIDTH, (f + 1) * WIDTH)


def image_rows(factor, z, side, chunks):
    rows = [factor[pl.ds(lax.rem(z + (e + Z), Z), 1), pl.ds(side, 1)].reshape(PART, WIDTH) for e in chunks]
    return jnp.concatenate(rows, axis=0)


def image_first(at, act_factor, grad_factor, mine, other, *outs):
    for f, factor in enumerate((act_factor, grad_factor)):
        rows = image_rows(factor, at[0], 1 - at[1], REDUCE[:4])
        for part, cols in ((mine, slice(0, HALF)), (other, slice(HALF, TOKENS))):
            image = dot_t(part[:, factor_columns(f)], rows).T.astype(bf16)
            for n, (group, k) in enumerate(PLACES[:3]):
                outs[group][k, f, :, cols] = image[n * PART : (n + 1) * PART]


def image_away(at, act_factor, grad_factor, mine, other, *outs):
    for f, factor in enumerate((act_factor, grad_factor)):
        rows = image_rows(factor, at[0], 1 - at[1], REDUCE[3:])
        for part, cols in ((mine, slice(0, HALF)), (other, slice(HALF, TOKENS))):
            image = dot_t(rows, part[:, factor_columns(f)]).astype(bf16)
            for n, (group, k) in enumerate(PLACES[3:]):
                outs[group - 2][k, f, :, cols] = image[n * PART : (n + 1) * PART]


def image_own(at, act_factor, grad_factor, mine, other, *outs):
    for f, factor in enumerate((act_factor, grad_factor)):
        rows = image_rows(factor, at[0], at[1], REDUCE)
        for part, cols in ((mine, slice(0, HALF)), (other, slice(HALF, TOKENS))):
            image = dot_t(rows, part[:, factor_columns(f)])
            for k in range(Z):
                outs[k][f, :, cols] = image[k * PART : (k + 1) * PART]
        square = sum(jnp.square(part[:, factor_columns(f)].astype(f32)) for part in (mine, other))
        outs[Z][f : f + 1] = jnp.sum(square, axis=0, keepdims=True)


def last_sum(own, away, up, down, squares, out):
    total = own[...] + away[0].astype(f32) + up[...].astype(f32) + down[...].astype(f32)
    total = total.astype(bf16)
    for n in range(2 * BLOCKS):
        f, block = divmod(n, BLOCKS)
        out[n * PART : (n + 1) * PART, :] = total[f, :, block * LANES : (block + 1) * LANES]
    row = lax.broadcasted_iota(jnp.int32, (EXTRA, LANES), 0)
    parts = jnp.zeros((EXTRA, LANES), f32)
    for f in range(2):
        rest = jnp.full((EXTRA, LANES), jnp.sum(squares[f : f + 1]))
        for k in range(3):
            part = rest.astype(bf16).astype(f32)
            parts = jnp.where(row == f * EXTRA // 2 + k, part, parts)
            rest = rest - part
    out[2 * BLOCKS * PART :, :] = parts.astype(bf16)


def changes(chunks, mine, other, f):
    def image(c):
        first = f * BLOCKS
        return jnp.concatenate([c[n * PART : (n + 1) * PART, :] for n in range(first, first + BLOCKS)], axis=1)

    image = jnp.concatenate([image(c) for c in chunks], axis=0)
    change = dot(image[:, :HALF], mine[:, factor_columns(f)])
    return change + dot(image[:, HALF:], other[:, factor_columns(f)])


def own_changes(mine, other, *refs):
    chunks, (out, squares) = refs[:Z], refs[Z:]
    for f in range(2):
        out[f] = changes(chunks, mine, other, f)
        squares[f : f + 1] = share_sum(chunks, f)


def share_sum(chunks, f):
    shares = sum(c[2 * BLOCKS * PART :, :].astype(f32) for c in chunks)
    half = EXTRA // 2
    return jnp.sum(shares[f * half : (f + 1) * half], axis=0, keepdims=True)


def update(at, act_factor, grad_factor, mine, other, own_change, squares, *refs):
    chunks, results, outs, sems = refs[:Z], refs[Z : Z + 2], refs[Z + 2 : Z + 4], refs[Z + 4]
    copies = [pltpu.make_async_copy(outs[f], results[f], sems.at[f]) for f in range(2)]
    for f, (factor, out) in enumerate(((act_factor, outs[0]), (grad_factor, outs[1]))):
        total = squares[1 - f : 2 - f] + share_sum(chunks, 1 - f)
        scale = total[:, :1] / (TOKENS * D) * (gram_scale / TOKENS)
        for side in range(YL):
            change = own_change[f] if side == 0 else changes(chunks, mine, other, f)
            half = pl.ds(at[1] if side == 0 else 1 - at[1], 1)
            for k, e in enumerate(GATHER):
                place = (pl.ds(lax.rem(at[0] + (e + Z), Z), 1), half)
                kept = factor[place].reshape(PART, WIDTH).astype(f32)
                new = keep_scale * kept - scale * change[k * PART : (k + 1) * PART]
                out[place] = new.astype(bf16).reshape(1, 1, PART, WIDTH)
        copies[f].start()
    for copy in copies:
        copy.wait()


def after(a, *others):
    for other in others:
        a = a + jnp.minimum(jnp.abs(other), 0)
    return a


def local(activations, cotangents, act_factor, grad_factor):
    core, z, yl = (lax.axis_index(name) for name in ("core", "z", "yl"))
    product = 4 * HALF * ROWS * WIDTH
    given = (activations, cotangents, act_factor, grad_factor)
    scratch = [pltpu.VMEM((HALF, ROWS), bf16), pltpu.VMEM((ROWS, WIDTH), bf16)] * 2
    scratch.append(pltpu.SemaphoreType.DMA((4,)))
    setup = dict(flops=product, memory=pltpu.HBM, scratch=scratch, room=58)
    (away,) = kernel_call(project, [((HALF, 2 * WIDTH), bf16)], *given, index=[1 - core], **setup)
    came = shift(away, "core", CORE)
    (total,) = kernel_call(project_own, [((HALF, 2 * WIDTH), bf16)], *given, came, index=[core], flops=product)
    group = X * YH
    chunks = (group, HALF // group, 2 * WIDTH)
    parts = lax.all_to_all(total.reshape(chunks), ("x", "yh"), 0, 0, tiled=True)
    (copies,) = kernel_call(project_sum, [(chunks, bf16)], parts)
    mine = lax.all_to_all(copies, ("x", "yh"), 0, 0, tiled=True).reshape(HALF, 2 * WIDTH)
    other = shift(mine, "core", CORE)

    factors = [f.reshape(Z, YL, PART, WIDTH) for f in (act_factor, grad_factor)]
    shape = (2, PART, TOKENS)
    sent = [((sum(g == group for g, _ in PLACES),) + shape, bf16) for group in range(5)]
    first = kernel_call(image_first, sent[:2], *factors, mine, other, index=[z, yl], flops=product // 2)
    away = first + kernel_call(image_away, sent[2:], *factors, mine, other, index=[z, yl], flops=product)
    away = [shift(a, "yl", YL) for a in away]
    *own, squares = kernel_call(
        image_own, [(shape, f32)] * Z + [((2, WIDTH), f32)], *factors, mine, other, index=[z, yl], flops=product
    )
    up = own[0] + away[0][0].astype(f32)
    down = own[1] + away[1][0].astype(f32)
    for step in (1, 2, 3):
        up = shift(up.astype(bf16), "z", Z, 1)
        up = own[2 * step] + away[step][1].astype(f32) + up.astype(f32)
        down = shift(down.astype(bf16), "z", Z, -1)
        if step < 3:
            down = own[2 * step + 1] + away[step + 1][0].astype(f32) + down.astype(f32)
    up = shift(up.astype(bf16), "z", Z, 1)
    shape = (2 * BLOCKS * PART + EXTRA, LANES)
    (up,) = kernel_call(last_sum, [(shape, bf16)], own[7], away[4], up, down, squares)

    down = up
    held, crossed = [up], [shift(up, "yl", YL)]
    for step in (1, 2, 3):
        if step == 3:
            up, down = after(up, crossed[0]), after(down, crossed[0])
        up, down = shift(up, "z", Z, 1), shift(down, "z", Z, -1)
        held += [up, down]
        crossed += [shift(up, "yl", YL), shift(down, "yl", YL)]
    up = shift(after(up, *crossed[1:3]), "z", Z, 1)
    held.append(up)
    crossed.append(shift(up, "yl", YL))
    changed, squares = kernel_call(
        own_changes, [((2, ROWS // YL, WIDTH), f32), ((2, LANES), f32)], mine, other, *held, flops=product
    )
    outs = kernel_call(
        update, [((Z, YL, PART, WIDTH), bf16)] * 2, *factors, mine, other, changed, squares, *crossed, index=[z, yl], flops=product,
        out_memory=pltpu.HBM, scratch=[pltpu.VMEM((Z, YL, PART, WIDTH), bf16)] * 2 + [pltpu.SemaphoreType.DMA((2,))],
    )
    return tuple(out.reshape(ROWS, WIDTH) for out in outs)


def solution(mesh):
    fine = Mesh(mesh.devices.reshape(X, YH, CORE, Z, YL), ROW + COL)
    return jax.shard_map(
        local,
        mesh=fine,
        in_specs=(P(None, ROW), P(None, ROW), P(ROW, COL), P(ROW, COL)),
        out_specs=(P(ROW, COL), P(ROW, COL)),
        check_vma=False,
    )
```
